32 devices in a mesh: depth: 4 (over y, x), row: 8 (over z, core).
Axes of the slice: x: 2, y: 2, z: 4, core: 2. Of those that a mesh axis runs over, the one named last changes fastest.
Arguments:
- field: float32 [2, 4, 4096, 4096], P(None, 'depth', 'row'), may hold values from -6 to 6
- hologram: float32 [4096, 4096], P('row'), may hold values from -6 to 6
- defocus: float32 [4], P('depth'), may hold values from 512 to 2048
Outputs:
- estimate: float32 [2, 4, 4096, 4096], P(None, 'depth', 'row')
The draws below stay inside these ranges and needn't reach their ends.
All inputs are finite; a program needn't handle non-finite values.
Results may differ from the reference program's by a relative error of at most 0.00045.
Values sent between devices are 32-bit elements; how exact they have to be, the bound alone decides.
No kernel may reach another device: no remote copies, remote signals or barrier semaphores. Data moves between devices by JAX's collectives and lax.ppermute only.
A program may use at most 320 MiB of HBM per device.

```python
import math
import jax
import jax.numpy as jnp
from jax import lax

N = 4096
ITERS = 1
PLANES = 4


def block_levels(key, dims, split, least, high):
    def one(position, parts):
        draws = jax.random.uniform(jax.random.fold_in(jax.random.fold_in(key, 6), position), (parts,), jnp.float32, least / len(split), high / len(split))
        return jnp.repeat(jnp.exp(draws), dims[position] // parts).reshape((-1,) + (1,) * (len(dims) - position - 1))

    factor_of = one(*split[0])
    for cut in split[1:]:
        factor_of = factor_of * one(*cut)
    return factor_of


def normal_values(rng, dims, deviation, bound, shards=(), kind=jnp.bfloat16):
    drawn = deviation * jax.random.normal(rng, dims, jnp.float32)
    if shards:
        drawn = drawn * block_levels(rng, dims, shards, -0.22, 0.18)
    return jnp.clip(drawn, -bound, bound).astype(kind)


def setup_inputs(seed: int = 0) -> dict:
    seeds = jax.random.split(jax.random.key(seed), 4)
    return {
        "field": normal_values(seeds[0], (2, PLANES, N, N), 1.0, 6.0, ((1, 4), (2, 8)), jnp.float32),
        "hologram": normal_values(seeds[1], (N, N), (PLANES ** 0.5), 6.0, ((0, 8),), jnp.float32),
        "defocus": jnp.clip(jnp.exp(math.log(2048.0) - 1.3862944 * jax.random.uniform(seeds[2], (PLANES,), jnp.float32) ** block_levels(seeds[2], (PLANES,), ((0, 4),), -0.2, 0.2)), 512.0, 2048.0),
    }


tv_step_size = 1.0 / 12.0
tv_sharpness = 0.25

def signed_squares(length_total):
    indices = jnp.arange(length_total, dtype=jnp.int32)
    centred = jnp.where(indices < length_total // 2, indices, indices - length_total)
    return (centred * centred).astype(jnp.float32)

def defocus_phase(depth_value, length_total):
    squares = signed_squares(length_total)
    grid_sum = (squares[:, None] + squares[None, :]) * (math.pi / (length_total * length_total))
    return depth_value * grid_sum

def forward_diff(values, axis_pos):
    extent = values.shape[axis_pos]
    shifted = jnp.concatenate([lax.slice_in_dim(values, 1, extent, axis=axis_pos), lax.slice_in_dim(values, extent - 1, extent, axis=axis_pos)], axis=axis_pos)
    return shifted - values

def backward_diff(values, axis_pos):
    extent = values.shape[axis_pos]
    shifted = jnp.concatenate([jnp.zeros_like(lax.slice_in_dim(values, 0, 1, axis=axis_pos)), lax.slice_in_dim(values, 0, extent - 1, axis=axis_pos)], axis=axis_pos)
    return values - shifted

def plane_flux(here_plane, ahead_plane):
    depth_diff = ahead_plane - here_plane
    row_diff = forward_diff(here_plane, 1)
    col_diff = forward_diff(here_plane, 2)
    magnitude = jnp.sqrt(lax.optimization_barrier(jnp.sum(depth_diff * depth_diff + row_diff * row_diff + col_diff * col_diff, axis=0)))
    factor = 1.0 / (1.0 + tv_sharpness * magnitude)
    return (depth_diff * factor, row_diff * factor, col_diff * factor)

def tv_shrink(moved_field):
    plane_total = moved_field.shape[1]

    def one_plane(index_z):
        here_plane = lax.dynamic_index_in_dim(moved_field, index_z, 1, keepdims=False)
        ahead_plane = lax.dynamic_index_in_dim(moved_field, jnp.minimum(index_z + 1, plane_total - 1), 1, keepdims=False)
        behind = lax.dynamic_index_in_dim(moved_field, jnp.maximum(index_z - 1, 0), 1, keepdims=False)
        flux_z, flux_y, flux_x = plane_flux(here_plane, ahead_plane)
        prior_z, prior_y, prior_x = plane_flux(behind, here_plane)
        prior_z = prior_z * (index_z > 0).astype(moved_field.dtype)
        divergence = flux_z - prior_z + backward_diff(flux_y, 1) + backward_diff(flux_x, 2)
        return here_plane + tv_step_size * divergence
    planes_out = lax.map(one_plane, jnp.arange(plane_total, dtype=jnp.int32))
    return jnp.moveaxis(planes_out, 0, 1)

def reference(field, hologram, defocus):
    length_total = field.shape[-1]
    plane_total = field.shape[1]
    zero_plane = jnp.zeros((length_total, length_total), jnp.float32)
    estimate = field
    for step_index in range(ITERS):

        def add_plane(summed, scan_item):
            real_part, imag_part, depth_value = scan_item
            spectrum = jnp.fft.fft2(lax.complex(real_part, imag_part))
            phase_table = defocus_phase(depth_value, length_total)
            return (summed + spectrum * lax.complex(jnp.cos(phase_table), -jnp.sin(phase_table)), None)
        summed, unused = lax.scan(add_plane, lax.complex(zero_plane, zero_plane), (estimate[0], estimate[1], defocus))
        image_real = jnp.real(jnp.fft.ifft2(summed))
        misfit = image_real - hologram
        misfit_spec = jnp.fft.fft2(lax.complex(misfit, jnp.zeros_like(misfit)))

        def adjoint_plane(depth_value):
            phase_table = defocus_phase(depth_value, length_total)
            plane_field = jnp.fft.ifft2(misfit_spec * lax.complex(jnp.cos(phase_table), jnp.sin(phase_table)))
            return (jnp.real(plane_field), jnp.imag(plane_field))
        grad_real, grad_imag = lax.map(adjoint_plane, defocus)
        gradient = jnp.stack([grad_real, grad_imag])
        moved_field = estimate - 1.0 / plane_total * gradient
        estimate = tv_shrink(moved_field)
    return estimate
```

```python
import math

import jax
import jax.numpy as jnp
import numpy as np
from jax import lax
from jax.experimental import pallas as pl
from jax.experimental.pallas import tpu as pltpu
from jax.sharding import Mesh, PartitionSpec as P

tv_step_size = 1.0 / 12.0
tv_sharpness = 0.25
LANES = 128
GROUPS = 4
PASSES = 2
VMEM_BYTES = 60 * 1024 * 1024
f32 = jnp.float32
bf16 = jnp.bfloat16


def c_add(u, v):
    return (u[0] + v[0], u[1] + v[1])


def c_sub(u, v):
    return (u[0] - v[0], u[1] - v[1])


def c_rot(u, num, den):
    num = num % den
    if num == 0:
        return u
    if 4 * num == den:
        return (-u[1], u[0])
    if 2 * num == den:
        return (-u[0], -u[1])
    if 4 * num == 3 * den:
        return (u[1], -u[0])
    if (8 * num) % den == 0:
        half = math.sqrt(0.5)
        eighth = (8 * num) // den
        plus = (u[0] + u[1]) * half
        minus = (u[0] - u[1]) * half
        if eighth == 1:
            return (minus, plus)
        if eighth == 3:
            return (-plus, minus)
        if eighth == 5:
            return (-minus, -plus)
        return (plus, -minus)
    cos = math.cos(2 * math.pi * num / den)
    sin = math.sin(2 * math.pi * num / den)
    return (u[0] * cos - u[1] * sin, u[0] * sin + u[1] * cos)


def dft4(v, sign):
    s, d = c_add(v[0], v[2]), c_sub(v[0], v[2])
    t, u = c_add(v[1], v[3]), c_sub(v[1], v[3])
    u = c_rot(u, sign, 4)
    return [c_add(s, t), c_add(d, u), c_sub(s, t), c_sub(d, u)]


def dft8(v, sign):
    even, odd = dft4(v[0::2], sign), dft4(v[1::2], sign)
    odd = [c_rot(odd[q], sign * q, 8) for q in range(4)]
    return [c_add(even[q], odd[q]) for q in range(4)] + [c_sub(even[q], odd[q]) for q in range(4)]


def real_rot(value, num, den):
    cos = math.cos(2 * math.pi * num / den)
    sin = math.sin(2 * math.pi * num / den)
    return (value * cos, value * sin)


def total(values):
    out = values[0]
    for value in values[1:]:
        out = out + value
    return out


def slab_forward(x, group):
    count = len(x)
    if group == 0 and count == 8:
        s0, d0, s1, d1 = x[0] + x[4], x[0] - x[4], x[2] + x[6], x[2] - x[6]
        s2, d2, s3, d3 = x[1] + x[5], x[1] - x[5], x[3] + x[7], x[3] - x[7]
        e0, e2, o0, o2 = s0 + s1, s0 - s1, s2 + s3, s2 - s3
        p1 = c_rot((d2, -d3), -1, 8)
        p3 = c_rot((d2, d3), -3, 8)
        return [(e0 + o0, e0 - o0), (d0 + p1[0], p1[1] - d1), (e2, -o2), (d0 + p3[0], d1 + p3[1])]
    if count == 8:
        w = [(x[0], None)] + [real_rot(x[j], -group * j, 32) for j in range(1, 8)]
        s, d = (x[0] + w[4][0], w[4][1]), (x[0] - w[4][0], -w[4][1])
        t, u = c_add(w[2], w[6]), c_rot(c_sub(w[2], w[6]), -1, 4)
        even = [c_add(s, t), c_add(d, u), c_sub(s, t), c_sub(d, u)]
        odd = dft4(w[1::2], -1)
        return [c_add(even[q], c_rot(odd[q], -q, 8)) for q in range(4)]
    outs = []
    for q in range(4):
        parts = [real_rot(x[j], -(group + 4 * q) * j, 32) for j in range(count)]
        outs.append((total([v[0] for v in parts]), total([v[1] for v in parts])))
    if group == 0:
        outs[0] = (total(x), total([x[j] if j % 2 == 0 else -x[j] for j in range(count)]))
    return outs


def slab_inverse(g, group, count):
    if group == 0:
        (top, alt), rest = g[0], g[1:]
        if count == 8:
            (a1, b1), (a2, b2), (a3, b3) = rest
            half = math.sqrt(0.5)
            p, m = top + alt, top - alt
            s13, d13 = a1 + a3, b1 - b3
            x0, x4 = p + a2 + s13, p + a2 - s13
            x2, x6 = p - a2 - d13, p - a2 + d13
            u = (a1 - a3) * half
            v = (b1 + b3) * half
            x1, x5 = m - b2 + (u - v), m - b2 - (u - v)
            x3, x7 = m + b2 - (u + v), m + b2 + (u + v)
            return [x0, x1, x2, x3, x4, x5, x6, x7]
        outs = []
        for j in range(count):
            terms = [c_rot(rest[q - 1], q * j, 8)[0] for q in range(1, 4)]
            outs.append((top + alt if j % 2 == 0 else top - alt) + total(terms))
        return outs
    if count == 8:
        even = dft4(g, 1)
        odd = dft4([c_rot(g[q], q, 8) for q in range(4)], 1)
        v = [even[0], odd[0], even[1], odd[1], even[2], odd[2], even[3], odd[3]]
        outs = [v[0][0]]
        for j in range(1, 8):
            cos = math.cos(2 * math.pi * group * j / 32)
            sin = math.sin(2 * math.pi * group * j / 32)
            outs.append(v[j][0] * cos - v[j][1] * sin)
        return outs
    outs = []
    for j in range(count):
        terms = [c_rot(g[q], (group + 4 * q) * j, 32)[0] for q in range(4)]
        outs.append(total(terms))
    return outs


def two_parts(value):
    high = value.astype(bf16)
    low = (value - high.astype(f32)).astype(bf16)
    return high, low


def dot(left, right):
    return jnp.dot(left, right, preferred_element_type=f32)


def host_parts(matrix):
    high = matrix.astype(np.float32).astype(jnp.bfloat16)
    low = (matrix - high.astype(np.float64)).astype(np.float32).astype(jnp.bfloat16)
    return high, low


def lane_tables():
    n = np.arange(LANES)
    angle = 2 * np.pi * (n[:, None] * n[None, :] % LANES) / LANES
    cos, sin = np.cos(angle), np.sin(angle)
    forward = np.block([[cos, -sin], [sin, cos]])
    inverse = np.block([[cos, sin], [-sin, cos]])
    stacked = []
    for matrix in (forward, inverse):
        high, low = host_parts(matrix)
        stacked.append(np.concatenate([high, high, low], axis=0))
    return stacked


def twiddle_table(length, tiles):
    k = np.arange(tiles)[:, None]
    n = np.arange(LANES)[None, :]
    angle = -2 * np.pi * (k * n % length) / length
    return np.stack([np.cos(angle), np.sin(angle)]).astype(np.float32)


def slot_bases(length):
    n = np.arange(LANES)[:, None]
    bases = np.zeros((16, 2 * LANES, 2 * LANES))
    freqs = np.zeros((16, 2 * LANES), np.int64)
    for group in range(GROUPS):
        for q in range(4):
            k = group + 4 * q
            slot = group * 4 + q
            if k == 0:
                column = 0
                for half, start in ((0, 0), (1, 16)):
                    rows = slice(half * LANES, (half + 1) * LANES)
                    for step in range(LANES // 2 + 1):
                        a = start + 32 * step
                        if a > length // 2:
                            continue
                        angle = 2 * np.pi * (a * n[:, 0] % length) / length
                        if a in (0, length // 2):
                            bases[slot, rows, column] = np.cos(angle) / np.sqrt(LANES)
                            freqs[slot, column] = a
                            column += 1
                            continue
                        bases[slot, rows, column] = np.cos(angle) * np.sqrt(2 / LANES)
                        bases[slot, rows, column + 1] = np.sin(angle) * np.sqrt(2 / LANES)
                        freqs[slot, column : column + 2] = a
                        column += 2
                assert column == 2 * LANES
                continue
            a = k + 32 * np.arange(LANES)[None, :]
            angle = 2 * np.pi * (a * n % length) / length
            cos, sin = np.cos(angle) / np.sqrt(LANES), np.sin(angle) / np.sqrt(LANES)
            bases[slot] = np.block([[cos, -sin], [sin, cos]])
            freqs[slot] = np.concatenate([a[0], a[0]])
    return bases.astype(np.float32), freqs


def chirp(depth_values, freqs, length):
    centred = np.where(freqs < length // 2, freqs, freqs - length)
    squares = (centred.astype(np.int64) ** 2).astype(np.int64)
    coarse = (squares // 2048 * 2048).astype(np.float32)
    fine = (squares % 2048).astype(np.float32)
    unit = 0.5 / (float(length) * float(length))
    whole = jnp.floor(depth_values * 2.0) * 0.5
    rest = depth_values - whole

    def turn(left, right):
        value = left * right * unit
        return value - jnp.floor(value)

    turns = turn(whole, coarse) + turn(whole, fine) + rest * (coarse * unit) + rest * (fine * unit)
    angle = (turns - jnp.floor(turns)) * (2.0 * math.pi)
    return jnp.cos(angle), jnp.sin(angle)


def lane_convolve(rows, load, store, work, parts, spec, forward_ref, inverse_ref, twiddle_ref, transfer):
    def put_parts(tile, row, pair):
        for at, value in enumerate(pair):
            high, low = two_parts(value)
            span = pl.ds(tile * rows + row, 16)
            parts[span, at * LANES : (at + 1) * LANES] = high
            parts[span, (2 + at) * LANES : (3 + at) * LANES] = low
            parts[span, (4 + at) * LANES : (5 + at) * LANES] = high

    def multiply(table_ref):
        step = min(512, 32 * rows)

        def body(i, carry):
            span = pl.ds(i * step, step)
            spec[span, :] = dot(parts[span, :], table_ref[...])
            return carry

        lax.fori_loop(0, 32 * rows // step, body, 0)

    def forward(i, carry):
        row = i * 16
        span = pl.ds(row, 16)
        for b in range(8):
            x = [load(8 * a + b, row) for a in range(4)]
            y = dft4(x, -1)
            for k in range(4):
                v = c_rot(y[k], -b * k, 32)
                work[0, k * 8 + b, span, :] = v[0]
                work[1, k * 8 + b, span, :] = v[1]
        for k in range(4):
            x = [(work[0, k * 8 + b, span, :], work[1, k * 8 + b, span, :]) for b in range(8)]
            y = dft8(x, -1)
            for m in range(8):
                tile = k + 4 * m
                tr, ti = twiddle_ref[0, tile : tile + 1, :], twiddle_ref[1, tile : tile + 1, :]
                re, im = y[m]
                put_parts(tile, row, (re * tr - im * ti, re * ti + im * tr))
        return carry

    lax.fori_loop(0, rows // 16, forward, 0)
    multiply(forward_ref)

    def middle(tile, carry):
        tr, ti = transfer(tile)
        for row in range(0, rows, 16):
            span = pl.ds(tile * rows + row, 16)
            re, im = spec[span, :LANES], spec[span, LANES:]
            put_parts(tile, row, (re * tr - im * ti, re * ti + im * tr))
        return carry

    lax.fori_loop(0, 32, middle, 0)
    multiply(inverse_ref)

    def inverse(i, carry):
        row = i * 16
        span = pl.ds(row, 16)
        for k in range(4):
            x = []
            for m in range(8):
                tile = k + 4 * m
                tr, ti = twiddle_ref[0, tile : tile + 1, :], twiddle_ref[1, tile : tile + 1, :]
                at = pl.ds(tile * rows + row, 16)
                re, im = spec[at, :LANES], spec[at, LANES:]
                x.append((re * tr + im * ti, im * tr - re * ti))
            y = dft8(x, 1)
            for b in range(8):
                v = c_rot(y[b], b * k, 32)
                work[0, k * 8 + b, span, :] = v[0]
                work[1, k * 8 + b, span, :] = v[1]
        for b in range(8):
            x = [(work[0, k * 8 + b, span, :], work[1, k * 8 + b, span, :]) for k in range(4)]
            y = dft4(x, 1)
            for a in range(4):
                store(8 * a + b, row, y[a])
        return carry

    lax.fori_loop(0, rows // 16, inverse, 0)


def lane_scratch(rows):
    return [
        pltpu.VMEM((2, 32, rows, LANES), f32),
        pltpu.VMEM((32 * rows, 6 * LANES), bf16),
        pltpu.VMEM((32 * rows, 2 * LANES), f32),
    ]


def params():
    return pltpu.CompilerParams(vmem_limit_bytes=VMEM_BYTES)


def whole_block(array):
    rank = array.ndim
    return pl.BlockSpec(array.shape, lambda *_: (0,) * rank)


def column_pass(plan, scalars, field, tables, transfer):
    rows = min(64, plan.rows_dev)
    level, chunk, cols = plan.level, plan.chunk, plan.cols_dev
    per_piece = cols // LANES
    n_out = level * PASSES

    def kernel(scal, f_ref, fwd, inv, twd, tra, *rest):
        outs, (work, parts, spec, staged) = rest[:n_out], rest[n_out:]

        def load(tile, row):
            at = slice(tile * LANES, (tile + 1) * LANES)
            return (f_ref[0, pl.ds(row, 16), at], f_ref[1, pl.ds(row, 16), at])

        def store(tile, row, value):
            staged[tile, 0, pl.ds(row, 16), :] = value[0]
            staged[tile, 1, pl.ds(row, 16), :] = value[1]

        def pick(tile):
            return tra[0, pl.ds(tile, 1), :], tra[1, pl.ds(tile, 1), :]

        lane_convolve(rows, load, store, work, parts, spec, fwd, inv, twd, pick)
        for part in range(PASSES):
            for s in range(level):
                first = jnp.bitwise_xor(scal[0], s) * per_piece + part * (chunk // LANES)
                for t in range(chunk // LANES):
                    for ri in range(2):
                        outs[part * level + s][ri, :, t * LANES : (t + 1) * LANES] = staged[first + t, ri]

    width = field.shape[-1]
    fixed = [tables["forward"], tables["inverse"], tables["twiddle"], transfer]
    return pl.pallas_call(
        kernel,
        grid_spec=pltpu.PrefetchScalarGridSpec(
            num_scalar_prefetch=1,
            grid=(plan.rows_dev // rows,),
            in_specs=[pl.BlockSpec((2, rows, width), lambda i, _: (0, i, 0))] + [whole_block(a) for a in fixed],
            out_specs=[pl.BlockSpec((2, rows, chunk), lambda i, _: (0, i, 0))] * n_out,
            scratch_shapes=lane_scratch(rows) + [pltpu.VMEM((32, 2, rows, LANES), f32)],
        ),
        out_shape=[jax.ShapeDtypeStruct((2, plan.rows_dev, chunk), f32)] * n_out,
        compiler_params=params(),
        cost_estimate=pl.CostEstimate(flops=13 * 10**9, bytes_accessed=34 * 10**6, transcendentals=0),
        name="column_pass",
    )(scalars, field, *fixed)


def slot_matrices(plan, bases, weights):
    kinds = weights.shape[1]
    size = 2 * LANES

    def kernel(b_ref, w_ref, high_ref, low_ref):
        basis = b_ref[0]
        for kind in range(kinds):
            scaled = basis * w_ref[0, kind : kind + 1, :]
            product = lax.dot_general(
                scaled,
                basis,
                (((1,), (1,)), ((), ())),
                precision=lax.Precision.HIGHEST,
                preferred_element_type=f32,
            )
            high, low = two_parts(product)
            high_ref[0, :, kind * size : (kind + 1) * size] = high
            low_ref[0, :, kind * size : (kind + 1) * size] = low

    shape = jax.ShapeDtypeStruct((16, size, kinds * size), bf16)
    return pl.pallas_call(
        kernel,
        grid=(16,),
        in_specs=[
            pl.BlockSpec((1, size, size), lambda i: (i, 0, 0)),
            pl.BlockSpec((1, kinds, size), lambda i: (i, 0, 0)),
        ],
        out_specs=[pl.BlockSpec((1, size, kinds * size), lambda i: (i, 0, 0))] * 2,
        out_shape=[shape, shape],
        compiler_params=params(),
        cost_estimate=pl.CostEstimate(flops=26 * 10**9, bytes_accessed=34 * 10**6, transcendentals=0),
        name="slot_matrices",
    )(bases, weights)


def row_forward(plan, scalars, phases, pieces, holos, high, low):
    level, chunk, count = plan.level, plan.chunk, plan.slab_tiles
    kinds = plan.planes * 2
    size = 2 * LANES
    half = count // 2

    def kernel(scal, phase, *refs):
        x_refs, (h0, h1, wh, wl, out, eh, el, eo) = refs[:level], refs[level:]
        flip = scal[3] != 0

        def tiles(first, second, row):
            left = [first(j, row) for j in range(half)]
            right = [second(j, row) for j in range(half)]
            lower = [jnp.where(flip, b, a) for a, b in zip(left, right)]
            upper = [jnp.where(flip, a, b) for a, b in zip(left, right)]
            return lower + upper

        for group in range(GROUPS):

            @pl.when(pl.program_id(0) == group)
            def _(group=group):
                def rows_of(i, carry):
                    row = i * 16
                    for kind in range(kinds):
                        t, ri = kind // 2, kind % 2

                        def first(j, row, t=t, ri=ri):
                            return x_refs[2 * t][ri, pl.ds(j * LANES + row, 16), :]

                        def second(j, row, t=t, ri=ri):
                            return x_refs[2 * t + 1][ri, pl.ds(j * LANES + row, 16), :]

                        outs = slab_forward(tiles(first, second, row), group)
                        for q in range(4):
                            for at in range(2):
                                a, b = two_parts(outs[q][at])
                                span = pl.ds(kind * size + at * LANES + row, 16)
                                eh[q, span, :] = a
                                el[q, span, :] = b
                    held = slab_forward(
                        tiles(
                            lambda j, row: h0[pl.ds(j * LANES + row, 16), :],
                            lambda j, row: h1[pl.ds(j * LANES + row, 16), :],
                            row,
                        ),
                        group,
                    )
                    for q in range(4):
                        for at in range(2):
                            eo[q, pl.ds(at * LANES + row, 16), :] = held[q][at]
                    return carry

                lax.fori_loop(0, LANES // 16, rows_of, 0)

        for q in range(4):
            value = dot(wh[q], eh[q]) + dot(wh[q], el[q]) + dot(wl[q], eh[q]) - eo[q]
            slot = pl.program_id(0) * 4 + q
            cos, sin = phase[0, slot], phase[1, slot]
            re, im = value[:LANES], value[LANES:]
            out[q, :LANES, :] = re * cos - im * sin
            out[q, LANES:, :] = re * sin + im * cos

    return pl.pallas_call(
        kernel,
        grid_spec=pltpu.PrefetchScalarGridSpec(
            num_scalar_prefetch=2,
            grid=(GROUPS,),
            in_specs=[whole_block(a) for a in pieces]
            + [whole_block(a) for a in holos]
            + [pl.BlockSpec((4, size, kinds * size), lambda g, *_: (g, 0, 0))] * 2,
            out_specs=pl.BlockSpec((4, size, chunk), lambda g, *_: (g, 0, 0)),
            scratch_shapes=[
                pltpu.VMEM((4, kinds * size, chunk), bf16),
                pltpu.VMEM((4, kinds * size, chunk), bf16),
                pltpu.VMEM((4, size, chunk), f32),
            ],
        ),
        out_shape=jax.ShapeDtypeStruct((16, size, chunk), f32),
        compiler_params=params(),
        cost_estimate=pl.CostEstimate(flops=13 * 10**9, bytes_accessed=60 * 10**6, transcendentals=0),
        name="row_forward",
    )(scalars, phases, *pieces, *holos, high, low)


def row_backward(plan, scalars, phases, misfit, high, low):
    level, chunk, count = plan.level, plan.chunk, plan.slab_tiles
    size = 2 * LANES
    piece = plan.piece

    def kernel(scal, phase, m_ref, wh, wl, *rest):
        outs, (mh, ml, field) = rest[:level], rest[level:]
        kind, step = pl.program_id(0), pl.program_id(1)

        @pl.when(kind == 0)
        def _():
            for q in range(4):
                slot = step * 4 + q
                cos, sin = phase[2, slot], phase[3, slot]
                re, im = m_ref[q, :LANES, :], m_ref[q, LANES:, :]
                for at, value in enumerate((re * cos - im * sin, re * sin + im * cos)):
                    a, b = two_parts(value)
                    mh[slot, at * LANES : (at + 1) * LANES, :] = a
                    ml[slot, at * LANES : (at + 1) * LANES, :] = b

        grads = []
        for q in range(4):
            slot = step * 4 + q
            grads.append(dot(wh[q], mh[slot]) + dot(wh[q], ml[slot]) + dot(wl[q], mh[slot]))
        for group in range(GROUPS):

            @pl.when(step == group)
            def _(group=group):
                for row in range(0, LANES, 16):
                    g = [(v[row : row + 16], v[LANES + row : LANES + row + 16]) for v in grads]
                    values = slab_inverse(g, group, count)
                    for j in range(count):
                        span = pl.ds(j * LANES + row, 16)
                        if group == 0:
                            field[span, :] = values[j]
                        else:
                            field[span, :] = field[span, :] + values[j]

        @pl.when(step == GROUPS - 1)
        def _():
            for s in range(level):
                other = jnp.bitwise_xor(scal[0], s)
                start = jnp.bitwise_and(other, 1) * plan.rows_dev + jnp.right_shift(other, 1) * piece
                outs[s][0] = field[pl.ds(pl.multiple_of(start, 16), piece), :]

    kinds = plan.planes * 2

    def weight_at(kind, step, scal, phase):
        return (step, 0, jnp.bitwise_xor(kind // 2, scal[1]) * 2 + kind % 2)

    return pl.pallas_call(
        kernel,
        grid_spec=pltpu.PrefetchScalarGridSpec(
            num_scalar_prefetch=2,
            grid=(kinds, GROUPS),
            in_specs=[
                pl.BlockSpec((4, size, chunk), lambda kind, step, *_: (jnp.where(kind == 0, step, GROUPS - 1), 0, 0)),
                pl.BlockSpec((4, size, size), weight_at),
                pl.BlockSpec((4, size, size), weight_at),
            ],
            out_specs=[pl.BlockSpec((1, piece, chunk), lambda kind, step, *_: (kind, 0, 0))] * level,
            scratch_shapes=[
                pltpu.VMEM((16, size, chunk), bf16),
                pltpu.VMEM((16, size, chunk), bf16),
                pltpu.VMEM((count * LANES, chunk), f32),
            ],
        ),
        out_shape=[jax.ShapeDtypeStruct((kinds, piece, chunk), f32)] * level,
        compiler_params=params(),
        cost_estimate=pl.CostEstimate(flops=13 * 10**9, bytes_accessed=60 * 10**6, transcendentals=0),
        name="row_backward",
    )(scalars, phases, misfit, high, low)


def step_pass(plan, scalars, pieces, held, tables, transfer):
    rows = min(64, plan.piece)
    level, chunk = plan.level, plan.chunk
    width = held.shape[-1]
    per_piece = plan.cols_dev // LANES
    n_in = level * PASSES
    flat = [piece for part in pieces for piece in part]
    scale = 1.0 / plan.planes

    def kernel(scal, *refs):
        g_refs, (h_ref, fwd, inv, twd, tra, out, work, parts, spec, staged) = refs[:n_in], refs[n_in:]
        for part in range(PASSES):
            for s in range(level):
                first = jnp.bitwise_xor(scal[0], s) * per_piece + part * (chunk // LANES)
                for t in range(chunk // LANES):
                    for ri in range(2):
                        staged[first + t, ri] = g_refs[part * level + s][ri, :, t * LANES : (t + 1) * LANES]

        def load(tile, row):
            return (staged[tile, 0, pl.ds(row, 16), :], staged[tile, 1, pl.ds(row, 16), :])

        def store(tile, row, value):
            at = slice(tile * LANES, (tile + 1) * LANES)
            for ri in range(2):
                before = h_ref[0, ri, pl.ds(row, 16), at]
                out[0, ri, pl.ds(row, 16), at] = before - scale * value[ri]

        def pick(tile):
            return tra[0, 0, pl.ds(tile, 1), :], tra[0, 1, pl.ds(tile, 1), :]

        lane_convolve(rows, load, store, work, parts, spec, fwd, inv, twd, pick)

    fixed = [tables["forward"], tables["inverse"], tables["twiddle"]]
    return pl.pallas_call(
        kernel,
        grid_spec=pltpu.PrefetchScalarGridSpec(
            num_scalar_prefetch=1,
            grid=(plan.planes, plan.piece // rows),
            in_specs=[pl.BlockSpec((2, rows, chunk), lambda p, i, _: (p, i, 0))] * n_in
            + [pl.BlockSpec((1, 2, rows, width), lambda p, i, scal: (jnp.bitwise_xor(p, scal[1]), 0, i, 0))]
            + [whole_block(a) for a in fixed]
            + [pl.BlockSpec((1, 2, 32, LANES), lambda p, i, _: (p, 0, 0, 0))],
            out_specs=pl.BlockSpec((1, 2, rows, width), lambda p, i, _: (p, 0, i, 0)),
            scratch_shapes=lane_scratch(rows) + [pltpu.VMEM((32, 2, rows, LANES), f32)],
        ),
        out_shape=jax.ShapeDtypeStruct((plan.planes, 2, plan.piece, width), f32),
        compiler_params=params(),
        cost_estimate=pl.CostEstimate(flops=13 * 10**9, bytes_accessed=51 * 10**6, transcendentals=0),
        name="step_pass",
    )(scalars, *flat, held, *fixed, transfer)


def shrink_pass(plan, scalars, moved, above, below):
    planes, width = plan.planes, moved.shape[-1]
    steps = plan.piece // 8
    cols = 1024

    def kernel(scal, cur, nxt, up, down, *rest):
        outs, (carry, est) = rest[:planes], rest[planes:]
        i = pl.program_id(0)
        last = i == steps - 1
        row_ids = lax.broadcasted_iota(jnp.int32, (8, cols), 0)
        lane_ids = lax.broadcasted_iota(jnp.int32, (8, cols), 1)
        end_row = jnp.logical_and(last, scal[5] != 0)

        def flux(tile, next_row, p, start):
            at_end = start + cols == width
            here = [tile(p, ri, start, cols) for ri in range(2)]
            dz, dy, dx = [], [], []
            for ri in range(2):
                if p + 1 < planes:
                    dz.append(tile(p + 1, ri, start, cols) - here[ri])
                follow = jnp.where(row_ids == 7, next_row(p, ri, start), pltpu.roll(here[ri], 7, 0))
                dy.append(follow - here[ri])
                if at_end:
                    ahead = jnp.where(lane_ids == cols - 1, here[ri], pltpu.roll(here[ri], cols - 1, 1))
                else:
                    joined = jnp.concatenate([here[ri], tile(p, ri, start + cols, LANES)], axis=1)
                    ahead = pltpu.roll(joined, cols + LANES - 1, 1)[:, :cols]
                dx.append(ahead - here[ri])
            squares = [v * v for v in dz + dy + dx]
            magnitude = jnp.sqrt(total(squares))
            factor = 1.0 / (1.0 + tv_sharpness * magnitude)
            return here, [v * factor for v in dz], [v * factor for v in dy], [v * factor for v in dx]

        @pl.when(i == 0)
        def _():
            for p in range(planes):
                for start in range(0, width, cols):
                    def tile(p, ri, at, wide):
                        return jnp.broadcast_to(up[p, ri, 0:1, at : at + wide], (8, wide))

                    def next_row(p, ri, at):
                        return cur[p, ri, 0:1, at : at + cols]

                    fy = flux(tile, next_row, p, start)[2]
                    for ri in range(2):
                        carry[p, ri, :, start : start + cols] = jnp.where(scal[4] != 0, 0.0, fy[ri])

        def tile(p, ri, at, wide):
            return cur[p, ri, :, at : at + wide]

        def next_row(p, ri, at):
            inner = nxt[p, ri, 0:1, at : at + cols]
            outer = down[p, ri, 0:1, at : at + cols]
            own = cur[p, ri, 7:8, at : at + cols]
            return jnp.where(end_row, own, jnp.where(last, outer, inner))

        prior_x = {}
        for start in range(0, width, cols):
            prior_z = None
            for p in range(planes):
                here, fz, fy, fx = flux(tile, next_row, p, start)
                for ri in range(2):
                    behind_y = jnp.where(row_ids == 0, carry[p, ri, 7:8, start : start + cols], pltpu.roll(fy[ri], 1, 0))
                    if start == 0:
                        behind_x = jnp.where(lane_ids == 0, 0.0, pltpu.roll(fx[ri], 1, 1))
                    else:
                        joined = jnp.concatenate([prior_x[p, ri], fx[ri]], axis=1)
                        behind_x = pltpu.roll(joined, 1, 1)[:, LANES:]
                    divergence = (fy[ri] - behind_y) + (fx[ri] - behind_x)
                    if fz:
                        divergence = divergence + fz[ri]
                    if prior_z:
                        divergence = divergence - prior_z[ri]
                    est[p, ri, :, start : start + cols] = here[ri] + tv_step_size * divergence
                    carry[p, ri, :, start : start + cols] = fy[ri]
                    prior_x[p, ri] = fx[ri][:, cols - LANES :]
                prior_z = fz
        for s in range(planes):
            outs[s][...] = est[jnp.bitwise_xor(scal[1], s)]

    return pl.pallas_call(
        kernel,
        grid_spec=pltpu.PrefetchScalarGridSpec(
            num_scalar_prefetch=1,
            grid=(steps,),
            in_specs=[
                pl.BlockSpec((planes, 2, 8, width), lambda i, _: (0, 0, i, 0)),
                pl.BlockSpec((planes, 2, 8, width), lambda i, _: (0, 0, jnp.minimum(i + 1, steps - 1), 0)),
                whole_block(above),
                whole_block(below),
            ],
            out_specs=[pl.BlockSpec((2, 8, width), lambda i, _: (0, i, 0))] * planes,
            scratch_shapes=[
                pltpu.VMEM((planes, 2, 8, width), f32),
                pltpu.VMEM((planes, 2, 8, width), f32),
            ],
        ),
        out_shape=[jax.ShapeDtypeStruct((2, plan.piece, width), f32)] * planes,
        compiler_params=params(),
        cost_estimate=pl.CostEstimate(flops=10**8, bytes_accessed=34 * 10**6, transcendentals=4 * 10**6),
        name="shrink_pass",
    )(scalars, moved, moved, above, below)


class Plan:
    def __init__(self, field_shape, depth, slabs):
        self.planes = depth
        self.slabs = slabs
        self.length = field_shape[-1]
        self.rows_dev = field_shape[-2]
        self.level = depth * 2
        self.cols_dev = self.length // self.level
        self.chunk = self.cols_dev // PASSES
        self.piece = self.rows_dev // depth
        self.slab_tiles = 2 * self.rows_dev // LANES


def swapped(value, axes, size, step):
    return lax.ppermute(value, axes, [(i, i ^ step) for i in range(size)])


def per_device(field, hologram, defocus):
    depth, slabs = lax.axis_size("depth"), lax.axis_size("slab")
    plan = Plan(field.shape, depth, slabs)
    length = plan.length
    d, z, c = lax.axis_index("depth"), lax.axis_index("slab"), lax.axis_index("core")
    me = d * 2 + c
    order = (z * 2 + c) * depth + d
    n_order = slabs * 2 * depth
    scalars = jnp.stack([me, d, z, c, (order == 0).astype(jnp.int32), (order == n_order - 1).astype(jnp.int32)])
    scalars = scalars.astype(jnp.int32)
    level_axes = ("depth", "core")

    forward, inverse = lane_tables()
    tables = {
        "forward": jnp.asarray(forward),
        "inverse": jnp.asarray(inverse),
        "twiddle": jnp.asarray(twiddle_table(length, 32)),
    }
    column_freqs = np.arange(32)[:, None] + 32 * np.arange(LANES)[None, :]
    cos, sin = chirp(defocus[0], column_freqs, length)
    transfer = jnp.stack([cos, -sin]) * (1.0 / length)

    own = field[:, 0]
    sent = column_pass(plan, scalars, own, tables, transfer)
    level = plan.level
    arrived = []
    for part in range(PASSES):
        group = sent[part * level : (part + 1) * level]
        arrived.append([group[0]] + [swapped(group[s], level_axes, level, s) for s in range(1, level)])

    depths = lax.all_gather(defocus, "depth", axis=0, tiled=True)
    ordered = depths[jnp.bitwise_xor(jnp.arange(depth, dtype=jnp.int32), d)]
    bases, freqs = slot_bases(length)
    cos, sin = chirp(ordered[None, :, None], freqs[:, None, :], length)
    weights = jnp.stack([cos, sin], axis=2).reshape(16, 2 * depth, 2 * LANES)
    high, low = slot_matrices(plan, jnp.asarray(bases), weights)

    slot_k = np.array([g + 4 * q for g in range(GROUPS) for q in range(4)])
    turns = (jnp.asarray(slot_k * plan.slab_tiles, jnp.int32) * z) % 32
    angle = turns.astype(f32) * (2.0 * math.pi / 32)
    unit = jnp.asarray(np.where(slot_k == 0, 1.0 / 32, 2.0 / 32), f32)
    phases = jnp.stack([jnp.cos(angle), -jnp.sin(angle), jnp.cos(angle) * unit, jnp.sin(angle) * unit])

    mine = lax.dynamic_slice_in_dim(hologram, me * plan.cols_dev, plan.cols_dev, 1)
    theirs = lax.dynamic_slice_in_dim(hologram, jnp.bitwise_xor(me, 1) * plan.cols_dev, plan.cols_dev, 1)
    theirs = swapped(theirs, "core", 2, 1)

    by_rows = own.reshape(2, depth, plan.piece, length)
    held = [lax.dynamic_index_in_dim(by_rows, jnp.bitwise_xor(d, s), 1, keepdims=False) for s in range(depth)]
    held = jnp.stack([held[0]] + [swapped(held[s], "depth", depth, s) for s in range(1, depth)])

    back = []
    for part in range(PASSES):
        span = slice(part * plan.chunk, (part + 1) * plan.chunk)
        partial = row_forward(plan, scalars, phases, arrived[part], [mine[:, span], theirs[:, span]], high, low)
        misfit = lax.psum(partial, "slab")
        group = row_backward(plan, scalars, phases, misfit, high, low)
        back.append([group[0]] + [swapped(group[s], level_axes, level, s) for s in range(1, level)])

    cos, sin = chirp(depths[:, None, None], column_freqs[None], length)
    transfer = jnp.stack([cos, sin], axis=1) * (1.0 / length)
    moved = step_pass(plan, scalars, back, held, tables, transfer)

    all_axes = ("depth", "slab", "core")
    device_at = [(i % depth) * (slabs * 2) + i // depth for i in range(n_order)]
    downward = [(device_at[i], device_at[i + 1]) for i in range(n_order - 1)]
    above = lax.ppermute(moved[:, :, -1:], all_axes, downward)
    below = lax.ppermute(moved[:, :, :1], all_axes, [(b, a) for a, b in downward])
    parts = shrink_pass(plan, scalars, moved, above, below)
    parts = [parts[0]] + [swapped(parts[s], "depth", depth, s) for s in range(1, depth)]
    stacked = jnp.stack(parts, axis=1)
    stacked = jnp.take(stacked, jnp.bitwise_xor(jnp.arange(depth, dtype=jnp.int32), d), axis=1)
    return stacked.reshape(field.shape)


def solution(mesh):
    depth, row = mesh.shape["depth"], mesh.shape["row"]
    split = Mesh(mesh.devices.reshape(depth, row // 2, 2), ("depth", "slab", "core"))
    rows = ("slab", "core")
    return jax.shard_map(
        per_device,
        mesh=split,
        in_specs=(P(None, "depth", rows, None), P(rows, None), P("depth")),
        out_specs=P(None, "depth", rows, None),
        check_vma=False,
    )
```

```python
import math

import jax
import jax.numpy as jnp
import numpy as np
from jax import lax
from jax.experimental import pallas as pl
from jax.experimental.pallas import tpu as pltpu
from jax.sharding import Mesh, PartitionSpec as P

tv_step_size = 1.0 / 12.0
tv_sharpness = 0.25
LANES = 128
GROUPS = 4
VMEM_BYTES = 60 * 1024 * 1024
f32 = jnp.float32
bf16 = jnp.bfloat16


def c_add(u, v):
    return (u[0] + v[0], u[1] + v[1])


def c_sub(u, v):
    return (u[0] - v[0], u[1] - v[1])


def c_rot(u, num, den):
    num = num % den
    if num == 0:
        return u
    if 4 * num == den:
        return (-u[1], u[0])
    if 2 * num == den:
        return (-u[0], -u[1])
    if 4 * num == 3 * den:
        return (u[1], -u[0])
    if (8 * num) % den == 0:
        half = math.sqrt(0.5)
        eighth = (8 * num) // den
        plus = (u[0] + u[1]) * half
        minus = (u[0] - u[1]) * half
        if eighth == 1:
            return (minus, plus)
        if eighth == 3:
            return (-plus, minus)
        if eighth == 5:
            return (-minus, -plus)
        return (plus, -minus)
    cos = math.cos(2 * math.pi * num / den)
    sin = math.sin(2 * math.pi * num / den)
    return (u[0] * cos - u[1] * sin, u[0] * sin + u[1] * cos)


def dft4(v, sign):
    s, d = c_add(v[0], v[2]), c_sub(v[0], v[2])
    t, u = c_add(v[1], v[3]), c_sub(v[1], v[3])
    u = c_rot(u, sign, 4)
    return [c_add(s, t), c_add(d, u), c_sub(s, t), c_sub(d, u)]


def dft8(v, sign):
    even, odd = dft4(v[0::2], sign), dft4(v[1::2], sign)
    odd = [c_rot(odd[q], sign * q, 8) for q in range(4)]
    return [c_add(even[q], odd[q]) for q in range(4)] + [c_sub(even[q], odd[q]) for q in range(4)]


def real_rot(value, num, den):
    cos = math.cos(2 * math.pi * num / den)
    sin = math.sin(2 * math.pi * num / den)
    return (value * cos, value * sin)


def total(values):
    out = values[0]
    for value in values[1:]:
        out = out + value
    return out


def slab_forward(x, group):
    count = len(x)
    if group == 0 and count == 8:
        s0, d0, s1, d1 = x[0] + x[4], x[0] - x[4], x[2] + x[6], x[2] - x[6]
        s2, d2, s3, d3 = x[1] + x[5], x[1] - x[5], x[3] + x[7], x[3] - x[7]
        e0, e2, o0, o2 = s0 + s1, s0 - s1, s2 + s3, s2 - s3
        p1 = c_rot((d2, -d3), -1, 8)
        p3 = c_rot((d2, d3), -3, 8)
        return [(e0 + o0, e0 - o0), (d0 + p1[0], p1[1] - d1), (e2, -o2), (d0 + p3[0], d1 + p3[1])]
    if count == 8:
        w = [(x[0], None)] + [real_rot(x[j], -group * j, 32) for j in range(1, 8)]
        s, d = (x[0] + w[4][0], w[4][1]), (x[0] - w[4][0], -w[4][1])
        t, u = c_add(w[2], w[6]), c_rot(c_sub(w[2], w[6]), -1, 4)
        even = [c_add(s, t), c_add(d, u), c_sub(s, t), c_sub(d, u)]
        odd = dft4(w[1::2], -1)
        return [c_add(even[q], c_rot(odd[q], -q, 8)) for q in range(4)]
    outs = []
    for q in range(4):
        parts = [real_rot(x[j], -(group + 4 * q) * j, 32) for j in range(count)]
        outs.append((total([v[0] for v in parts]), total([v[1] for v in parts])))
    if group == 0:
        outs[0] = (total(x), total([x[j] if j % 2 == 0 else -x[j] for j in range(count)]))
    return outs


def slab_inverse(g, group, count):
    if group == 0:
        (top, alt), rest = g[0], g[1:]
        if count == 8:
            (a1, b1), (a2, b2), (a3, b3) = rest
            half = math.sqrt(0.5)
            p, m = top + alt, top - alt
            s13, d13 = a1 + a3, b1 - b3
            x0, x4 = p + a2 + s13, p + a2 - s13
            x2, x6 = p - a2 - d13, p - a2 + d13
            u = (a1 - a3) * half
            v = (b1 + b3) * half
            x1, x5 = m - b2 + (u - v), m - b2 - (u - v)
            x3, x7 = m + b2 - (u + v), m + b2 + (u + v)
            return [x0, x1, x2, x3, x4, x5, x6, x7]
        outs = []
        for j in range(count):
            terms = [c_rot(rest[q - 1], q * j, 8)[0] for q in range(1, 4)]
            outs.append((top + alt if j % 2 == 0 else top - alt) + total(terms))
        return outs
    if count == 8:
        even = dft4(g, 1)
        odd = dft4([c_rot(g[q], q, 8) for q in range(4)], 1)
        v = [even[0], odd[0], even[1], odd[1], even[2], odd[2], even[3], odd[3]]
        outs = [v[0][0]]
        for j in range(1, 8):
            cos = math.cos(2 * math.pi * group * j / 32)
            sin = math.sin(2 * math.pi * group * j / 32)
            outs.append(v[j][0] * cos - v[j][1] * sin)
        return outs
    outs = []
    for j in range(count):
        terms = [c_rot(g[q], (group + 4 * q) * j, 32)[0] for q in range(4)]
        outs.append(total(terms))
    return outs


def two_parts(value):
    high = value.astype(bf16)
    low = (value - high.astype(f32)).astype(bf16)
    return high, low


def dot(left, right):
    return jnp.dot(left, right, preferred_element_type=f32)


def host_parts(matrix):
    high = matrix.astype(np.float32).astype(jnp.bfloat16)
    low = (matrix - high.astype(np.float64)).astype(np.float32).astype(jnp.bfloat16)
    return high, low


def lane_tables():
    n = np.arange(LANES)
    angle = 2 * np.pi * (n[:, None] * n[None, :] % LANES) / LANES
    cos, sin = np.cos(angle), np.sin(angle)
    forward = np.block([[cos, -sin], [sin, cos]])
    inverse = np.block([[cos, sin], [-sin, cos]])
    stacked = []
    for matrix in (forward, inverse):
        high, low = host_parts(matrix)
        stacked.append(np.concatenate([high, high, low], axis=0))
    return stacked


def twiddle_table(length, tiles):
    k = np.arange(tiles)[:, None]
    n = np.arange(LANES)[None, :]
    angle = -2 * np.pi * (k * n % length) / length
    return np.stack([np.cos(angle), np.sin(angle)]).astype(np.float32)


def slot_bases(length):
    n = np.arange(LANES)[:, None]
    bases = np.zeros((16, 2 * LANES, 2 * LANES))
    freqs = np.zeros((16, 2 * LANES), np.int64)
    for group in range(GROUPS):
        for q in range(4):
            k = group + 4 * q
            slot = group * 4 + q
            if k == 0:
                column = 0
                for half, start in ((0, 0), (1, 16)):
                    rows = slice(half * LANES, (half + 1) * LANES)
                    for step in range(LANES // 2 + 1):
                        a = start + 32 * step
                        if a > length // 2:
                            continue
                        angle = 2 * np.pi * (a * n[:, 0] % length) / length
                        if a in (0, length // 2):
                            bases[slot, rows, column] = np.cos(angle) / np.sqrt(LANES)
                            freqs[slot, column] = a
                            column += 1
                            continue
                        bases[slot, rows, column] = np.cos(angle) * np.sqrt(2 / LANES)
                        bases[slot, rows, column + 1] = np.sin(angle) * np.sqrt(2 / LANES)
                        freqs[slot, column : column + 2] = a
                        column += 2
                assert column == 2 * LANES
                continue
            a = k + 32 * np.arange(LANES)[None, :]
            angle = 2 * np.pi * (a * n % length) / length
            cos, sin = np.cos(angle) / np.sqrt(LANES), np.sin(angle) / np.sqrt(LANES)
            bases[slot] = np.block([[cos, -sin], [sin, cos]])
            freqs[slot] = np.concatenate([a[0], a[0]])
    return bases.astype(np.float32), freqs


def chirp(depth_values, freqs, length):
    centred = np.where(freqs < length // 2, freqs, freqs - length)
    squares = (centred.astype(np.int64) ** 2).astype(np.int64)
    coarse = (squares // 2048 * 2048).astype(np.float32)
    fine = (squares % 2048).astype(np.float32)
    unit = 0.5 / (float(length) * float(length))
    whole = jnp.floor(depth_values * 2.0) * 0.5
    rest = depth_values - whole

    def turn(left, right):
        value = left * right * unit
        return value - jnp.floor(value)

    turns = turn(whole, coarse) + turn(whole, fine) + rest * (coarse * unit) + rest * (fine * unit)
    angle = (turns - jnp.floor(turns)) * (2.0 * math.pi)
    return jnp.cos(angle), jnp.sin(angle)


def lane_convolve(rows, load, store, work, parts, spec, forward_ref, inverse_ref, twiddle_ref, transfer):
    def put_parts(tile, row, pair):
        for at, value in enumerate(pair):
            high, low = two_parts(value)
            span = pl.ds(tile * rows + row, 16)
            parts[span, at * LANES : (at + 1) * LANES] = high
            parts[span, (2 + at) * LANES : (3 + at) * LANES] = low
            parts[span, (4 + at) * LANES : (5 + at) * LANES] = high

    def forward(i, carry):
        row = i * 16
        span = pl.ds(row, 16)
        for b in range(8):
            x = [load(8 * a + b, row) for a in range(4)]
            y = dft4(x, -1)
            for k in range(4):
                v = c_rot(y[k], -b * k, 32)
                work[0, k * 8 + b, span, :] = v[0]
                work[1, k * 8 + b, span, :] = v[1]
        for k in range(4):
            x = [(work[0, k * 8 + b, span, :], work[1, k * 8 + b, span, :]) for b in range(8)]
            y = dft8(x, -1)
            for m in range(8):
                tile = k + 4 * m
                tr, ti = twiddle_ref[0, tile : tile + 1, :], twiddle_ref[1, tile : tile + 1, :]
                re, im = y[m]
                put_parts(tile, row, (re * tr - im * ti, re * ti + im * tr))
        return carry

    lax.fori_loop(0, rows // 16, forward, 0)
    batch = max(1, min(4, 256 // rows))

    def middle(i, carry):
        span = pl.ds(i * batch * rows, batch * rows)
        value = dot(parts[span, :], forward_ref[...])
        pieces = []
        for t in range(batch):
            tr, ti = transfer(i * batch + t)
            re = value[t * rows : (t + 1) * rows, :LANES]
            im = value[t * rows : (t + 1) * rows, LANES:]
            pieces.append(jnp.concatenate([re * tr - im * ti, re * ti + im * tr], axis=1))
        high, low = two_parts(jnp.concatenate(pieces, axis=0))
        spec[span, :] = dot(jnp.concatenate([high, low, high], axis=1), inverse_ref[...])
        return carry

    lax.fori_loop(0, 32 // batch, middle, 0, unroll=2)

    def inverse(i, carry):
        row = i * 16
        span = pl.ds(row, 16)
        for k in range(4):
            x = []
            for m in range(8):
                tile = k + 4 * m
                tr, ti = twiddle_ref[0, tile : tile + 1, :], twiddle_ref[1, tile : tile + 1, :]
                at = pl.ds(tile * rows + row, 16)
                re, im = spec[at, :LANES], spec[at, LANES:]
                x.append((re * tr + im * ti, im * tr - re * ti))
            y = dft8(x, 1)
            for b in range(8):
                v = c_rot(y[b], b * k, 32)
                work[0, k * 8 + b, span, :] = v[0]
                work[1, k * 8 + b, span, :] = v[1]
        for b in range(8):
            x = [(work[0, k * 8 + b, span, :], work[1, k * 8 + b, span, :]) for k in range(4)]
            y = dft4(x, 1)
            for a in range(4):
                store(8 * a + b, row, y[a])
        return carry

    lax.fori_loop(0, rows // 16, inverse, 0)


def lane_scratch(rows):
    return [
        pltpu.VMEM((2, 32, rows, LANES), f32),
        pltpu.VMEM((32 * rows, 6 * LANES), bf16),
        pltpu.VMEM((32 * rows, 2 * LANES), f32),
    ]


def params():
    return pltpu.CompilerParams(vmem_limit_bytes=VMEM_BYTES)


def whole_block(array):
    rank = array.ndim
    return pl.BlockSpec(array.shape, lambda *_: (0,) * rank)


def column_pass(plan, field, tables, transfer):
    rows = min(64, plan.rows_dev)
    level, count = plan.level, len(plan.chunks)

    def kernel(f_ref, fwd, inv, twd, tra, *rest):
        outs, (work, parts, spec) = rest[:count], rest[count:]

        def load(tile, row):
            at = slice(tile * LANES, (tile + 1) * LANES)
            return (f_ref[0, pl.ds(row, 16), at], f_ref[1, pl.ds(row, 16), at])

        def store(tile, row, value):
            owner, part, at = plan.place_of(tile)
            outs[part][owner, 0, pl.ds(row, 16), at] = value[0]
            outs[part][owner, 1, pl.ds(row, 16), at] = value[1]

        def pick(tile):
            return tra[0, pl.ds(tile, 1), :], tra[1, pl.ds(tile, 1), :]

        lane_convolve(rows, load, store, work, parts, spec, fwd, inv, twd, pick)

    width = field.shape[-1]
    fixed = [tables["forward"], tables["inverse"], tables["twiddle"], transfer]
    return pl.pallas_call(
        kernel,
        grid=(plan.rows_dev // rows,),
        in_specs=[pl.BlockSpec((2, rows, width), lambda i: (0, i, 0))] + [whole_block(a) for a in fixed],
        out_specs=[pl.BlockSpec((level, 2, rows, w), lambda i: (0, 0, i, 0)) for w in plan.chunks],
        scratch_shapes=lane_scratch(rows),
        out_shape=[jax.ShapeDtypeStruct((level, 2, plan.rows_dev, w), f32) for w in plan.chunks],
        compiler_params=params(),
        cost_estimate=pl.CostEstimate(flops=13 * 10**9, bytes_accessed=34 * 10**6, transcendentals=0),
        name="column_pass",
    )(field, *fixed)


def slot_matrices(plan, bases, weights):
    kinds = weights.shape[1]
    size = 2 * LANES

    def kernel(b_ref, w_ref, high_ref, low_ref):
        basis = b_ref[0]
        for kind in range(kinds):
            scaled = basis * w_ref[0, kind : kind + 1, :]
            product = lax.dot_general(
                scaled,
                basis,
                (((1,), (1,)), ((), ())),
                precision=lax.Precision.HIGHEST,
                preferred_element_type=f32,
            )
            high, low = two_parts(product)
            high_ref[0, :, kind * size : (kind + 1) * size] = high
            low_ref[0, :, kind * size : (kind + 1) * size] = low

    shape = jax.ShapeDtypeStruct((16, size, kinds * size), bf16)
    return pl.pallas_call(
        kernel,
        grid=(16,),
        in_specs=[
            pl.BlockSpec((1, size, size), lambda i: (i, 0, 0)),
            pl.BlockSpec((1, kinds, size), lambda i: (i, 0, 0)),
        ],
        out_specs=[pl.BlockSpec((1, size, kinds * size), lambda i: (i, 0, 0))] * 2,
        out_shape=[shape, shape],
        compiler_params=params(),
        cost_estimate=pl.CostEstimate(flops=26 * 10**9, bytes_accessed=34 * 10**6, transcendentals=0),
        name="slot_matrices",
    )(bases, weights)


def row_forward(plan, phases, pieces, holos, high, low):
    count = plan.slab_tiles
    chunk = pieces.shape[-1]
    kinds = plan.planes * 2
    size = 2 * LANES
    half = count // 2

    def kernel(phase, x_ref, h_ref, wh, wl, out, eh, el, eo):
        for group in range(GROUPS):

            @pl.when(pl.program_id(0) == group)
            def _(group=group):
                def rows_of(i, carry):
                    row = i * 16
                    for kind in range(kinds):
                        t, ri = kind // 2, kind % 2

                        x = []
                        for j in range(count):
                            span = pl.ds((j % half) * LANES + row, 16)
                            x.append(x_ref[2 * t + j // half, ri, span, :])
                        outs = slab_forward(x, group)
                        for q in range(4):
                            for at in range(2):
                                a, b = two_parts(outs[q][at])
                                span = pl.ds(kind * size + at * LANES + row, 16)
                                eh[q, span, :] = a
                                el[q, span, :] = b
                    x = []
                    for j in range(count):
                        span = pl.ds((j % half) * LANES + row, 16)
                        x.append(h_ref[j // half, span, :])
                    held = slab_forward(x, group)
                    for q in range(4):
                        for at in range(2):
                            eo[q, pl.ds(at * LANES + row, 16), :] = held[q][at]
                    return carry

                lax.fori_loop(0, LANES // 16, rows_of, 0)

        for q in range(4):
            value = dot(wh[q], eh[q]) + dot(wh[q], el[q]) + dot(wl[q], eh[q]) - eo[q]
            slot = pl.program_id(0) * 4 + q
            cos, sin = phase[0, slot], phase[1, slot]
            re, im = value[:LANES], value[LANES:]
            out[q, :LANES, :] = re * cos - im * sin
            out[q, LANES:, :] = re * sin + im * cos

    return pl.pallas_call(
        kernel,
        grid_spec=pltpu.PrefetchScalarGridSpec(
            num_scalar_prefetch=1,
            grid=(GROUPS,),
            in_specs=[whole_block(pieces), whole_block(holos)]
            + [pl.BlockSpec((4, size, kinds * size), lambda g, *_: (g, 0, 0))] * 2,
            out_specs=pl.BlockSpec((4, size, chunk), lambda g, *_: (g, 0, 0)),
            scratch_shapes=[
                pltpu.VMEM((4, kinds * size, chunk), bf16),
                pltpu.VMEM((4, kinds * size, chunk), bf16),
                pltpu.VMEM((4, size, chunk), f32),
            ],
        ),
        out_shape=jax.ShapeDtypeStruct((16, size, chunk), f32),
        compiler_params=params(),
        cost_estimate=pl.CostEstimate(flops=13 * 10**9, bytes_accessed=60 * 10**6, transcendentals=0),
        name="row_forward",
    )(phases, pieces, holos, high, low)


def row_backward(plan, phases, misfit, high, low):
    level, count = plan.level, plan.slab_tiles
    chunk = misfit.shape[-1]
    size = 2 * LANES
    piece = plan.piece

    def kernel(phase, m_ref, wh, wl, out, mh, ml, field):
        kind, step = pl.program_id(0), pl.program_id(1)

        @pl.when(kind == 0)
        def _():
            for q in range(4):
                slot = step * 4 + q
                cos, sin = phase[2, slot], phase[3, slot]
                re, im = m_ref[q, :LANES, :], m_ref[q, LANES:, :]
                for at, value in enumerate((re * cos - im * sin, re * sin + im * cos)):
                    a, b = two_parts(value)
                    mh[slot, at * LANES : (at + 1) * LANES, :] = a
                    ml[slot, at * LANES : (at + 1) * LANES, :] = b

        grads = []
        for q in range(4):
            slot = step * 4 + q
            grads.append(dot(wh[q], mh[slot]) + dot(wh[q], ml[slot]) + dot(wl[q], mh[slot]))
        for group in range(GROUPS):

            @pl.when(step == group)
            def _(group=group):
                for row in range(0, LANES, 16):
                    g = [(v[row : row + 16], v[LANES + row : LANES + row + 16]) for v in grads]
                    values = slab_inverse(g, group, count)
                    for j in range(count):
                        span = pl.ds(j * LANES + row, 16)
                        if group == 0:
                            field[span, :] = values[j]
                        else:
                            field[span, :] = field[span, :] + values[j]

        @pl.when(step == GROUPS - 1)
        def _():
            for s in range(level):
                start = (s % 2) * plan.rows_dev + (s // 2) * piece
                out[s, 0] = field[start : start + piece, :]

    kinds = plan.planes * 2

    return pl.pallas_call(
        kernel,
        grid_spec=pltpu.PrefetchScalarGridSpec(
            num_scalar_prefetch=1,
            grid=(kinds, GROUPS),
            in_specs=[
                pl.BlockSpec((4, size, chunk), lambda kind, step, _: (jnp.where(kind == 0, step, GROUPS - 1), 0, 0)),
                pl.BlockSpec((4, size, size), lambda kind, step, _: (step, 0, kind)),
                pl.BlockSpec((4, size, size), lambda kind, step, _: (step, 0, kind)),
            ],
            out_specs=pl.BlockSpec((level, 1, piece, chunk), lambda kind, step, _: (0, kind, 0, 0)),
            scratch_shapes=[
                pltpu.VMEM((16, size, chunk), bf16),
                pltpu.VMEM((16, size, chunk), bf16),
                pltpu.VMEM((count * LANES, chunk), f32),
            ],
        ),
        out_shape=jax.ShapeDtypeStruct((level, kinds, piece, chunk), f32),
        compiler_params=params(),
        cost_estimate=pl.CostEstimate(flops=13 * 10**9, bytes_accessed=60 * 10**6, transcendentals=0),
        name="row_backward",
    )(phases, misfit, high, low)


def step_pass(plan, pieces, held, tables, transfer):
    rows = min(64, plan.piece)
    level, count = plan.level, len(plan.chunks)
    width = held.shape[-1]
    scale = 1.0 / plan.planes

    def kernel(*refs):
        g_refs, (h_ref, fwd, inv, twd, tra, out, work, parts, spec) = refs[:count], refs[count:]

        def load(tile, row):
            owner, part, at = plan.place_of(tile)
            return (g_refs[part][owner, 0, pl.ds(row, 16), at], g_refs[part][owner, 1, pl.ds(row, 16), at])

        def store(tile, row, value):
            at = slice(tile * LANES, (tile + 1) * LANES)
            for ri in range(2):
                before = h_ref[0, ri, pl.ds(row, 16), at]
                out[0, ri, pl.ds(row, 16), at] = before - scale * value[ri]

        def pick(tile):
            return tra[0, 0, pl.ds(tile, 1), :], tra[0, 1, pl.ds(tile, 1), :]

        lane_convolve(rows, load, store, work, parts, spec, fwd, inv, twd, pick)

    fixed = [tables["forward"], tables["inverse"], tables["twiddle"]]
    return pl.pallas_call(
        kernel,
        grid=(plan.planes, plan.piece // rows),
        in_specs=[pl.BlockSpec((level, 2, rows, w), lambda p, i: (0, p, i, 0)) for w in plan.chunks]
        + [pl.BlockSpec((1, 2, rows, width), lambda p, i: (p, 0, i, 0))]
        + [whole_block(a) for a in fixed]
        + [pl.BlockSpec((1, 2, 32, LANES), lambda p, i: (p, 0, 0, 0))],
        out_specs=pl.BlockSpec((1, 2, rows, width), lambda p, i: (p, 0, i, 0)),
        scratch_shapes=lane_scratch(rows),
        out_shape=jax.ShapeDtypeStruct((plan.planes, 2, plan.piece, width), f32),
        compiler_params=params(),
        cost_estimate=pl.CostEstimate(flops=13 * 10**9, bytes_accessed=51 * 10**6, transcendentals=0),
        name="step_pass",
    )(*pieces, held, *fixed, transfer)


def shrink_pass(plan, scalars, moved, above, below, begin, steps):
    planes, width = plan.planes, moved.shape[-1]
    tiles = plan.piece // 8
    at_top, at_bottom = begin == 0, begin + steps == tiles
    cols = 1024

    def kernel(scal, cur, nxt, up, down, *rest):
        outs, (carry, est) = rest[:planes], rest[planes:]
        i = pl.program_id(0)
        last = jnp.logical_and(i == steps - 1, at_bottom)
        row_ids = lax.broadcasted_iota(jnp.int32, (8, cols), 0)
        lane_ids = lax.broadcasted_iota(jnp.int32, (8, cols), 1)
        end_row = jnp.logical_and(last, scal[1] != 0)

        def flux(tile, next_row, p, start):
            at_end = start + cols == width
            here = [tile(p, ri, start, cols) for ri in range(2)]
            dz, dy, dx = [], [], []
            for ri in range(2):
                if p + 1 < planes:
                    dz.append(tile(p + 1, ri, start, cols) - here[ri])
                follow = jnp.where(row_ids == 7, next_row(p, ri, start), pltpu.roll(here[ri], 7, 0))
                dy.append(follow - here[ri])
                if at_end:
                    ahead = jnp.where(lane_ids == cols - 1, here[ri], pltpu.roll(here[ri], cols - 1, 1))
                else:
                    joined = jnp.concatenate([here[ri], tile(p, ri, start + cols, LANES)], axis=1)
                    ahead = pltpu.roll(joined, cols + LANES - 1, 1)[:, :cols]
                dx.append(ahead - here[ri])
            squares = [v * v for v in dz + dy + dx]
            magnitude = jnp.sqrt(total(squares))
            factor = 1.0 / (1.0 + tv_sharpness * magnitude)
            return here, [v * factor for v in dz], [v * factor for v in dy], [v * factor for v in dx]

        @pl.when(i == 0)
        def _():
            for p in range(planes):
                for start in range(0, width, cols):
                    def tile(p, ri, at, wide):
                        line = slice(0, 1) if at_top else slice(7, 8)
                        return jnp.broadcast_to(up[p, ri, line, at : at + wide], (8, wide))

                    def next_row(p, ri, at):
                        return cur[p, ri, 0:1, at : at + cols]

                    fy = flux(tile, next_row, p, start)[2]
                    for ri in range(2):
                        if at_top:
                            fy[ri] = jnp.where(scal[0] != 0, 0.0, fy[ri])
                        carry[p, ri, :, start : start + cols] = fy[ri]

        def tile(p, ri, at, wide):
            return cur[p, ri, :, at : at + wide]

        def next_row(p, ri, at):
            inner = nxt[p, ri, 0:1, at : at + cols]
            outer = down[p, ri, 0:1, at : at + cols]
            own = cur[p, ri, 7:8, at : at + cols]
            return jnp.where(end_row, own, jnp.where(last, outer, inner))

        prior_x = {}
        for start in range(0, width, cols):
            prior_z = None
            for p in range(planes):
                here, fz, fy, fx = flux(tile, next_row, p, start)
                for ri in range(2):
                    behind_y = jnp.where(row_ids == 0, carry[p, ri, 7:8, start : start + cols], pltpu.roll(fy[ri], 1, 0))
                    if start == 0:
                        behind_x = jnp.where(lane_ids == 0, 0.0, pltpu.roll(fx[ri], 1, 1))
                    else:
                        joined = jnp.concatenate([prior_x[p, ri], fx[ri]], axis=1)
                        behind_x = pltpu.roll(joined, 1, 1)[:, LANES:]
                    divergence = (fy[ri] - behind_y) + (fx[ri] - behind_x)
                    if fz:
                        divergence = divergence + fz[ri]
                    if prior_z:
                        divergence = divergence - prior_z[ri]
                    est[p, ri, :, start : start + cols] = here[ri] + tv_step_size * divergence
                    carry[p, ri, :, start : start + cols] = fy[ri]
                    prior_x[p, ri] = fx[ri][:, cols - LANES :]
                prior_z = fz
        for s in range(planes):
            outs[s][...] = est[jnp.bitwise_xor(scal[2], s)]
    return pl.pallas_call(
        kernel,
        grid_spec=pltpu.PrefetchScalarGridSpec(
            num_scalar_prefetch=1,
            grid=(steps,),
            in_specs=[
                pl.BlockSpec((planes, 2, 8, width), lambda i, _: (0, 0, begin + i, 0)),
                pl.BlockSpec((planes, 2, 8, width), lambda i, _: (0, 0, jnp.minimum(begin + i + 1, tiles - 1), 0)),
                whole_block(above) if at_top else pl.BlockSpec((planes, 2, 8, width), lambda i, _: (0, 0, begin - 1, 0)),
                whole_block(below),
            ],
            out_specs=[pl.BlockSpec((2, 8, width), lambda i, _: (0, i, 0))] * planes,
            scratch_shapes=[
                pltpu.VMEM((planes, 2, 8, width), f32),
                pltpu.VMEM((planes, 2, 8, width), f32),
            ],
        ),
        out_shape=[jax.ShapeDtypeStruct((2, steps * 8, width), f32)] * planes,
        compiler_params=params(),
        cost_estimate=pl.CostEstimate(flops=10**8, bytes_accessed=9 * 10**6, transcendentals=10**6),
        name="shrink_pass",
    )(scalars, moved, moved, above if at_top else moved, below)


def place_rows(plan, scalars, pieces, begin, result):
    rows, width = pieces[0].shape[-2:]
    count = len(pieces)
    given = [] if result is None else [result]

    def kernel(scal, *refs):
        sources, out, sems = refs[:count], refs[count + len(given)], refs[-1]
        ri = pl.program_id(0)
        copies = []
        for s in range(count):
            start = jnp.bitwise_xor(scal[2], s) * plan.piece + begin
            span = pl.ds(pl.multiple_of(start, 8), rows)
            copies.append(pltpu.make_async_copy(sources[s], out.at[pl.ds(ri, 1), span, :], sems.at[s]))
        for copy in copies:
            copy.start()
        for copy in copies:
            copy.wait()

    return pl.pallas_call(
        kernel,
        grid_spec=pltpu.PrefetchScalarGridSpec(
            num_scalar_prefetch=1,
            grid=(2,),
            in_specs=[pl.BlockSpec((1, rows, width), lambda ri, _: (ri, 0, 0))] * count
            + [pl.BlockSpec(memory_space=pl.ANY)] * len(given),
            out_specs=pl.BlockSpec(memory_space=pl.ANY),
            scratch_shapes=[pltpu.SemaphoreType.DMA((count,))],
        ),
        out_shape=jax.ShapeDtypeStruct((2, plan.rows_dev, width), f32),
        input_output_aliases={count + 1: 0} if given else {},
        compiler_params=pltpu.CompilerParams(vmem_limit_bytes=8 * 1024 * 1024),
        cost_estimate=pl.CostEstimate(flops=0, bytes_accessed=9 * 10**6, transcendentals=0),
        name="place_rows",
    )(scalars, *pieces, *given)


class Plan:
    def __init__(self, field_shape, depth, slabs):
        self.planes = depth
        self.slabs = slabs
        self.length = field_shape[-1]
        self.rows_dev = field_shape[-2]
        self.level = depth * 2
        self.cols_dev = self.length // self.level
        tiles = self.cols_dev // LANES
        self.chunks = [LANES] * tiles
        self.starts = [sum(self.chunks[:i]) for i in range(len(self.chunks))]
        self.piece = self.rows_dev // depth
        self.slab_tiles = 2 * self.rows_dev // LANES

    def place_of(self, tile):
        owner, inner = divmod(tile * LANES, self.cols_dev)
        part = max(i for i, start in enumerate(self.starts) if start <= inner)
        first = inner - self.starts[part]
        return owner, part, slice(first, first + LANES)


def swapped(value, axes, size, step):
    return lax.ppermute(value, axes, [(i, i ^ step) for i in range(size)])


def after(value, *others):
    return lax.optimization_barrier((value,) + others)[0]


def halving_steps(size):
    steps = []
    step = 1
    while step < size:
        steps.append(step)
        step = step * 2
    return steps


def scatter_step(value, axis, size, position, step, others):
    upper = jnp.bitwise_and(position, step) != 0
    half = value.shape[0] // 2
    kept = jnp.where(upper, value[half:], value[:half])
    given = jnp.where(upper, value[:half], value[half:])
    return kept + swapped(after(given, *others), axis, size, step)


def gather_step(value, axis, size, position, step, others):
    upper = jnp.bitwise_and(position, step) != 0
    other = swapped(after(value, *others), axis, size, step)
    return jnp.concatenate([jnp.where(upper, other, value), jnp.where(upper, value, other)])


def exchanged(value, axes):
    return lax.all_to_all(value, axes, 0, 0, tiled=True)


def per_device(field, hologram, defocus):
    depth, slabs = lax.axis_size("depth"), lax.axis_size("slab")
    plan = Plan(field.shape, depth, slabs)
    length = plan.length
    d, z, c = lax.axis_index("depth"), lax.axis_index("slab"), lax.axis_index("core")
    me = d * 2 + c
    order = (z * 2 + c) * depth + d
    n_order = slabs * 2 * depth
    ends = jnp.stack([(order == 0).astype(jnp.int32), (order == n_order - 1).astype(jnp.int32), d.astype(jnp.int32)])
    level_axes = ("depth", "core")

    forward, inverse = lane_tables()
    tables = {
        "forward": jnp.asarray(forward),
        "inverse": jnp.asarray(inverse),
        "twiddle": jnp.asarray(twiddle_table(length, 32)),
    }
    column_freqs = np.arange(32)[:, None] + 32 * np.arange(LANES)[None, :]
    cos, sin = chirp(defocus[0], column_freqs, length)
    transfer = jnp.stack([cos, -sin]) * (1.0 / length)

    ordered = jnp.concatenate([defocus] + [swapped(defocus, "depth", depth, s) for s in range(1, depth)])
    depths = ordered[jnp.bitwise_xor(jnp.arange(depth, dtype=jnp.int32), d)]

    own = field[:, 0]
    quarters = 4
    by_rows = own.reshape(2, depth, quarters, plan.piece // quarters, length)
    early = jnp.moveaxis(by_rows[:, :, 0], 1, 0)
    own, early, depths = lax.optimization_barrier((own, early, depths))
    held = [exchanged(early, "depth")]

    sent = column_pass(plan, own, tables, transfer)
    bases, freqs = slot_bases(length)
    cos, sin = chirp(depths[None, :, None], freqs[:, None, :], length)
    weights = jnp.stack([cos, sin], axis=2).reshape(16, 2 * depth, 2 * LANES)
    weights, bases, *sent = lax.optimization_barrier((weights, jnp.asarray(bases), *sent))
    high, low = slot_matrices(plan, bases, weights)

    slot_k = np.array([g + 4 * q for g in range(GROUPS) for q in range(4)])
    turns = (jnp.asarray(slot_k * plan.slab_tiles, jnp.int32) * z) % 32
    angle = turns.astype(f32) * (2.0 * math.pi / 32)
    unit = jnp.asarray(np.where(slot_k == 0, 1.0 / 32, 2.0 / 32), f32)
    phases = jnp.stack([jnp.cos(angle), -jnp.sin(angle), jnp.cos(angle) * unit, jnp.sin(angle) * unit])

    mine = lax.dynamic_slice_in_dim(hologram, me * plan.cols_dev, plan.cols_dev, 1)
    theirs = lax.dynamic_slice_in_dim(hologram, jnp.bitwise_xor(me, 1) * plan.cols_dev, plan.cols_dev, 1)
    theirs = swapped(theirs, "core", 2, 1)
    holos = jnp.where(c == 0, jnp.stack([mine, theirs]), jnp.stack([theirs, mine]))

    count = len(plan.chunks)

    def forward_stage(value, part, others):
        start = plan.starts[part]
        here = holos[:, :, start : start + plan.chunks[part]]
        return row_forward(plan, phases, after(value, *others), here, high, low)

    def backward_stage(value, part, others):
        return row_backward(plan, phases, after(value, *others), high, low)

    def sum_stage(function, step):
        return lambda value, part, others: function(value, "slab", slabs, z, step, others)

    halvings = halving_steps(slabs)
    stages = [forward_stage]
    stages += [sum_stage(scatter_step, step) for step in halvings]
    stages += [sum_stage(gather_step, step) for step in reversed(halvings)]
    stages += [backward_stage]

    queue = list(sent) + [None] * (quarters - 1)
    state = [None] * count
    before, back = [held[0]], []
    slot = 0
    while len(back) < count:
        others, before = before, []
        if queue:
            value = queue.pop(0)
            if value is None:
                value = after(by_rows[:, :, len(held)], *others)
                held.append(exchanged(jnp.moveaxis(value, 1, 0), "depth"))
                before.append(held[-1])
            else:
                before.append(exchanged(after(value, *others), level_axes))
                if slot < count:
                    state[slot] = before[-1]
                else:
                    back.append(before[-1])
        for part in range(count):
            stage = slot - (part + 1)
            if 0 <= stage < len(stages):
                state[part] = stages[stage](state[part], part, others)
                before.append(state[part])
                if stage == len(stages) - 1:
                    queue.append(state[part])
        if slot == 0:
            before += [high, low]
        slot += 1

    held = jnp.stack(held, axis=2).reshape(depth, 2, plan.piece, length)
    cos, sin = chirp(depths[:, None, None], column_freqs[None], length)
    transfer = jnp.stack([cos, sin], axis=1) * (1.0 / length)
    moved = step_pass(plan, back, held, tables, transfer)

    all_axes = ("depth", "slab", "core")
    device_at = [(i % depth) * (slabs * 2) + i // depth for i in range(n_order)]
    downward = [(device_at[i], device_at[i + 1]) for i in range(n_order - 1)]
    above = lax.ppermute(moved[:, :, -1:], all_axes, downward)
    below = lax.ppermute(moved[:, :, :1], all_axes, [(b, a) for a, b in downward])
    tiles = plan.piece // 8
    steps = max(1, tiles // 4)
    result = None
    for begin in range(0, tiles, steps):
        parts = shrink_pass(plan, ends, moved, above, below, begin, steps)
        parts = [parts[0]] + [swapped(parts[s], "depth", depth, s) for s in range(1, depth)]
        result = place_rows(plan, ends, parts, begin * 8, result)
    return result.reshape(field.shape)


def solution(mesh):
    depth, row = mesh.shape["depth"], mesh.shape["row"]
    split = Mesh(mesh.devices.reshape(depth, row // 2, 2), ("depth", "slab", "core"))
    rows = ("slab", "core")
    return jax.shard_map(
        per_device,
        mesh=split,
        in_specs=(P(None, "depth", rows, None), P(rows, None), P("depth")),
        out_specs=P(None, "depth", rows, None),
        check_vma=False,
    )
```

```python
import math

import jax
import jax.numpy as jnp
import numpy as np
from jax import lax
from jax.experimental import pallas as pl
from jax.experimental.pallas import tpu as pltpu
from jax.sharding import Mesh, PartitionSpec as P

tv_step_size = 1.0 / 12.0
tv_sharpness = 0.25
LANES = 128
GROUPS = 4
VMEM_BYTES = 60 * 1024 * 1024
f32 = jnp.float32
bf16 = jnp.bfloat16


def c_add(u, v):
    return (u[0] + v[0], u[1] + v[1])


def c_sub(u, v):
    return (u[0] - v[0], u[1] - v[1])


def c_rot(u, num, den):
    num = num % den
    if num == 0:
        return u
    if 4 * num == den:
        return (-u[1], u[0])
    if 2 * num == den:
        return (-u[0], -u[1])
    if 4 * num == 3 * den:
        return (u[1], -u[0])
    if (8 * num) % den == 0:
        half = math.sqrt(0.5)
        eighth = (8 * num) // den
        plus = (u[0] + u[1]) * half
        minus = (u[0] - u[1]) * half
        if eighth == 1:
            return (minus, plus)
        if eighth == 3:
            return (-plus, minus)
        if eighth == 5:
            return (-minus, -plus)
        return (plus, -minus)
    cos = math.cos(2 * math.pi * num / den)
    sin = math.sin(2 * math.pi * num / den)
    return (u[0] * cos - u[1] * sin, u[0] * sin + u[1] * cos)


def dft4(v, sign):
    s, d = c_add(v[0], v[2]), c_sub(v[0], v[2])
    t, u = c_add(v[1], v[3]), c_sub(v[1], v[3])
    u = c_rot(u, sign, 4)
    return [c_add(s, t), c_add(d, u), c_sub(s, t), c_sub(d, u)]


def dft8(v, sign):
    even, odd = dft4(v[0::2], sign), dft4(v[1::2], sign)
    odd = [c_rot(odd[q], sign * q, 8) for q in range(4)]
    return [c_add(even[q], odd[q]) for q in range(4)] + [c_sub(even[q], odd[q]) for q in range(4)]


def real_rot(value, num, den):
    cos = math.cos(2 * math.pi * num / den)
    sin = math.sin(2 * math.pi * num / den)
    return (value * cos, value * sin)


def total(values):
    out = values[0]
    for value in values[1:]:
        out = out + value
    return out


def slab_forward(x, group):
    count = len(x)
    if group == 0 and count == 8:
        s0, d0, s1, d1 = x[0] + x[4], x[0] - x[4], x[2] + x[6], x[2] - x[6]
        s2, d2, s3, d3 = x[1] + x[5], x[1] - x[5], x[3] + x[7], x[3] - x[7]
        e0, e2, o0, o2 = s0 + s1, s0 - s1, s2 + s3, s2 - s3
        p1 = c_rot((d2, -d3), -1, 8)
        p3 = c_rot((d2, d3), -3, 8)
        return [(e0 + o0, e0 - o0), (d0 + p1[0], p1[1] - d1), (e2, -o2), (d0 + p3[0], d1 + p3[1])]
    if count == 8:
        w = [(x[0], None)] + [real_rot(x[j], -group * j, 32) for j in range(1, 8)]
        s, d = (x[0] + w[4][0], w[4][1]), (x[0] - w[4][0], -w[4][1])
        t, u = c_add(w[2], w[6]), c_rot(c_sub(w[2], w[6]), -1, 4)
        even = [c_add(s, t), c_add(d, u), c_sub(s, t), c_sub(d, u)]
        odd = dft4(w[1::2], -1)
        return [c_add(even[q], c_rot(odd[q], -q, 8)) for q in range(4)]
    outs = []
    for q in range(4):
        parts = [real_rot(x[j], -(group + 4 * q) * j, 32) for j in range(count)]
        outs.append((total([v[0] for v in parts]), total([v[1] for v in parts])))
    if group == 0:
        outs[0] = (total(x), total([x[j] if j % 2 == 0 else -x[j] for j in range(count)]))
    return outs


def slab_inverse(g, group, count):
    if group == 0:
        (top, alt), rest = g[0], g[1:]
        if count == 8:
            (a1, b1), (a2, b2), (a3, b3) = rest
            half = math.sqrt(0.5)
            p, m = top + alt, top - alt
            s13, d13 = a1 + a3, b1 - b3
            x0, x4 = p + a2 + s13, p + a2 - s13
            x2, x6 = p - a2 - d13, p - a2 + d13
            u = (a1 - a3) * half
            v = (b1 + b3) * half
            x1, x5 = m - b2 + (u - v), m - b2 - (u - v)
            x3, x7 = m + b2 - (u + v), m + b2 + (u + v)
            return [x0, x1, x2, x3, x4, x5, x6, x7]
        outs = []
        for j in range(count):
            terms = [c_rot(rest[q - 1], q * j, 8)[0] for q in range(1, 4)]
            outs.append((top + alt if j % 2 == 0 else top - alt) + total(terms))
        return outs
    if count == 8:
        even = dft4(g, 1)
        odd = dft4([c_rot(g[q], q, 8) for q in range(4)], 1)
        v = [even[0], odd[0], even[1], odd[1], even[2], odd[2], even[3], odd[3]]
        outs = [v[0][0]]
        for j in range(1, 8):
            cos = math.cos(2 * math.pi * group * j / 32)
            sin = math.sin(2 * math.pi * group * j / 32)
            outs.append(v[j][0] * cos - v[j][1] * sin)
        return outs
    outs = []
    for j in range(count):
        terms = [c_rot(g[q], (group + 4 * q) * j, 32)[0] for q in range(4)]
        outs.append(total(terms))
    return outs


def two_parts(value):
    high = value.astype(bf16)
    low = (value - high.astype(f32)).astype(bf16)
    return high, low


def dot(left, right):
    return jnp.dot(left, right, preferred_element_type=f32)


def host_parts(matrix):
    high = matrix.astype(np.float32).astype(jnp.bfloat16)
    low = (matrix - high.astype(np.float64)).astype(np.float32).astype(jnp.bfloat16)
    return high, low


def lane_tables():
    n = np.arange(LANES)
    angle = 2 * np.pi * (n[:, None] * n[None, :] % LANES) / LANES
    cos, sin = np.cos(angle), np.sin(angle)
    forward = np.block([[cos, -sin], [sin, cos]])
    inverse = np.block([[cos, sin], [-sin, cos]])
    stacked = []
    for matrix in (forward, inverse):
        high, low = host_parts(matrix)
        stacked.append(np.concatenate([high, high, low], axis=0))
    return stacked


def twiddle_table(length, tiles):
    k = np.arange(tiles)[:, None]
    n = np.arange(LANES)[None, :]
    angle = -2 * np.pi * (k * n % length) / length
    return np.stack([np.cos(angle), np.sin(angle)]).astype(np.float32)


def slot_bases(length):
    n = np.arange(LANES)[:, None]
    bases = np.zeros((16, 2 * LANES, 2 * LANES))
    freqs = np.zeros((16, 2 * LANES), np.int64)
    for group in range(GROUPS):
        for q in range(4):
            k = group + 4 * q
            slot = group * 4 + q
            if k == 0:
                column = 0
                for half, start in ((0, 0), (1, 16)):
                    rows = slice(half * LANES, (half + 1) * LANES)
                    for step in range(LANES // 2 + 1):
                        a = start + 32 * step
                        if a > length // 2:
                            continue
                        angle = 2 * np.pi * (a * n[:, 0] % length) / length
                        if a in (0, length // 2):
                            bases[slot, rows, column] = np.cos(angle) / np.sqrt(LANES)
                            freqs[slot, column] = a
                            column += 1
                            continue
                        bases[slot, rows, column] = np.cos(angle) * np.sqrt(2 / LANES)
                        bases[slot, rows, column + 1] = np.sin(angle) * np.sqrt(2 / LANES)
                        freqs[slot, column : column + 2] = a
                        column += 2
                assert column == 2 * LANES
                continue
            a = k + 32 * np.arange(LANES)[None, :]
            angle = 2 * np.pi * (a * n % length) / length
            cos, sin = np.cos(angle) / np.sqrt(LANES), np.sin(angle) / np.sqrt(LANES)
            bases[slot] = np.block([[cos, -sin], [sin, cos]])
            freqs[slot] = np.concatenate([a[0], a[0]])
    return bases.astype(np.float32), freqs


def chirp(depth_values, freqs, length):
    centred = np.where(freqs < length // 2, freqs, freqs - length)
    squares = (centred.astype(np.int64) ** 2).astype(np.int64)
    coarse = (squares // 2048 * 2048).astype(np.float32)
    fine = (squares % 2048).astype(np.float32)
    unit = 0.5 / (float(length) * float(length))
    whole = jnp.floor(depth_values * 2.0) * 0.5
    rest = depth_values - whole

    def turn(left, right):
        value = left * right * unit
        return value - jnp.floor(value)

    turns = turn(whole, coarse) + turn(whole, fine) + rest * (coarse * unit) + rest * (fine * unit)
    angle = (turns - jnp.floor(turns)) * (2.0 * math.pi)
    return jnp.cos(angle), jnp.sin(angle)


def lane_convolve(rows, load, store, scratch, forward_ref, inverse_ref, twiddle_ref, transfer):
    ahead, behind = scratch[0], scratch[1]
    parts, spec = scratch[2:4], scratch[4:6]

    def twiddle(tile):
        return twiddle_ref[0, tile : tile + 1, :], twiddle_ref[1, tile : tile + 1, :]

    def forward(chunk):
        row, out = chunk * 16, parts[chunk % 2]
        for b in range(8):
            x = [load(8 * a + b, row) for a in range(4)]
            y = dft4(x, -1)
            for k in range(4):
                v = c_rot(y[k], -b * k, 32)
                ahead[0, k * 8 + b] = v[0]
                ahead[1, k * 8 + b] = v[1]
        for k in range(4):
            y = dft8([(ahead[0, k * 8 + b], ahead[1, k * 8 + b]) for b in range(8)], -1)
            for m in range(8):
                tile = k + 4 * m
                tr, ti = twiddle(tile)
                re, im = y[m]
                span = slice(tile * 16, tile * 16 + 16)
                for at, value in enumerate((re * tr - im * ti, re * ti + im * tr)):
                    high, low = two_parts(value)
                    out[span, at * LANES : (at + 1) * LANES] = high
                    out[span, (2 + at) * LANES : (3 + at) * LANES] = low
                    out[span, (4 + at) * LANES : (5 + at) * LANES] = high

    def middle(chunk):
        taken, out = parts[chunk % 2], spec[chunk % 2]
        for first in range(0, 32, 16):
            span = slice(first * 16, first * 16 + 256)
            value = dot(taken[span, :], forward_ref[...])
            pieces = []
            for t in range(16):
                tr, ti = transfer(first + t)
                re, im = value[t * 16 : t * 16 + 16, :LANES], value[t * 16 : t * 16 + 16, LANES:]
                pieces.append(jnp.concatenate([re * tr - im * ti, re * ti + im * tr], axis=1))
            high, low = two_parts(jnp.concatenate(pieces, axis=0))
            out[span, :] = dot(jnp.concatenate([high, low, high], axis=1), inverse_ref[...])

    def inverse(chunk):
        row, taken = chunk * 16, spec[chunk % 2]
        for k in range(4):
            x = []
            for m in range(8):
                tile = k + 4 * m
                tr, ti = twiddle(tile)
                span = slice(tile * 16, tile * 16 + 16)
                re, im = taken[span, :LANES], taken[span, LANES:]
                x.append((re * tr + im * ti, im * tr - re * ti))
            y = dft8(x, 1)
            for b in range(8):
                v = c_rot(y[b], b * k, 32)
                behind[0, k * 8 + b] = v[0]
                behind[1, k * 8 + b] = v[1]
        for b in range(8):
            y = dft4([(behind[0, k * 8 + b], behind[1, k * 8 + b]) for k in range(4)], 1)
            for a in range(4):
                store(8 * a + b, row, y[a])

    count = rows // 16
    for t in range(count + 2):
        if t < count:
            forward(t)
        if 0 <= t - 1 < count:
            middle(t - 1)
        if 0 <= t - 2 < count:
            inverse(t - 2)


def lane_scratch():
    work = pltpu.VMEM((2, 32, 16, LANES), f32)
    parts = pltpu.VMEM((512, 6 * LANES), bf16)
    spec = pltpu.VMEM((512, 2 * LANES), f32)
    return [work, work, parts, parts, spec, spec]


def params():
    return pltpu.CompilerParams(vmem_limit_bytes=VMEM_BYTES)


def whole_block(array):
    rank = array.ndim
    return pl.BlockSpec(array.shape, lambda *_: (0,) * rank)


def column_pass(plan, field, tables, transfer):
    rows = min(64, plan.rows_dev)
    level, count = plan.level, len(plan.chunks)

    def kernel(f_ref, fwd, inv, twd, tra, *rest):
        outs, scratch = rest[:count], rest[count:]

        def load(tile, row):
            at = slice(tile * LANES, (tile + 1) * LANES)
            return (f_ref[0, pl.ds(row, 16), at], f_ref[1, pl.ds(row, 16), at])

        def store(tile, row, value):
            owner, part, at = plan.place_of(tile)
            outs[part][owner, 0, pl.ds(row, 16), at] = value[0]
            outs[part][owner, 1, pl.ds(row, 16), at] = value[1]

        def pick(tile):
            return tra[0, tile : tile + 1, :], tra[1, tile : tile + 1, :]

        lane_convolve(rows, load, store, scratch, fwd, inv, twd, pick)

    width = field.shape[-1]
    fixed = [tables["forward"], tables["inverse"], tables["twiddle"], transfer]
    return pl.pallas_call(
        kernel,
        grid=(plan.rows_dev // rows,),
        in_specs=[pl.BlockSpec((2, rows, width), lambda i: (0, i, 0))] + [whole_block(a) for a in fixed],
        out_specs=[pl.BlockSpec((level, 2, rows, w), lambda i: (0, 0, i, 0)) for w in plan.chunks],
        scratch_shapes=lane_scratch(),
        out_shape=[jax.ShapeDtypeStruct((level, 2, plan.rows_dev, w), f32) for w in plan.chunks],
        compiler_params=params(),
        cost_estimate=pl.CostEstimate(flops=13 * 10**9, bytes_accessed=34 * 10**6, transcendentals=0),
        name="column_pass",
    )(field, *fixed)


def cut_rows(plan, field, part, parts):
    rows, width = plan.piece // parts, field.shape[-1]

    def kernel(x_ref, out_ref):
        out_ref[0] = x_ref[...]

    return pl.pallas_call(
        kernel,
        grid=(plan.planes,),
        in_specs=[pl.BlockSpec((2, rows, width), lambda p: (0, p * parts + part, 0))],
        out_specs=pl.BlockSpec((1, 2, rows, width), lambda p: (p, 0, 0, 0)),
        out_shape=jax.ShapeDtypeStruct((plan.planes, 2, rows, width), f32),
        compiler_params=params(),
        cost_estimate=pl.CostEstimate(flops=0, bytes_accessed=9 * 10**6, transcendentals=0),
        name="cut_rows",
    )(field)


def slot_matrices(plan, bases, weights):
    kinds = weights.shape[1]
    size = 2 * LANES

    def kernel(b_ref, w_ref, high_ref, low_ref):
        basis = b_ref[0]
        for kind in range(kinds):
            scaled = basis * w_ref[0, kind : kind + 1, :]
            product = lax.dot_general(
                scaled,
                basis,
                (((1,), (1,)), ((), ())),
                precision=lax.Precision.HIGHEST,
                preferred_element_type=f32,
            )
            high, low = two_parts(product)
            high_ref[0, :, kind * size : (kind + 1) * size] = high
            low_ref[0, :, kind * size : (kind + 1) * size] = low

    shape = jax.ShapeDtypeStruct((16, size, kinds * size), bf16)
    return pl.pallas_call(
        kernel,
        grid=(16,),
        in_specs=[
            pl.BlockSpec((1, size, size), lambda i: (i, 0, 0)),
            pl.BlockSpec((1, kinds, size), lambda i: (i, 0, 0)),
        ],
        out_specs=[pl.BlockSpec((1, size, kinds * size), lambda i: (i, 0, 0))] * 2,
        out_shape=[shape, shape],
        compiler_params=params(),
        cost_estimate=pl.CostEstimate(flops=26 * 10**9, bytes_accessed=34 * 10**6, transcendentals=0),
        name="slot_matrices",
    )(bases, weights)


def row_forward(plan, phases, pieces, holos, high, low):
    count = plan.slab_tiles
    chunk = pieces.shape[-1]
    kinds = plan.planes * 2
    size = 2 * LANES
    half = count // 2

    def kernel(phase, x_ref, h_ref, wh, wl, out, eh, el, eo):
        for group in range(GROUPS):

            @pl.when(pl.program_id(0) == group)
            def _(group=group):
                def rows_of(i, carry):
                    row = i * 16
                    for kind in range(kinds):
                        t, ri = kind // 2, kind % 2

                        x = []
                        for j in range(count):
                            span = pl.ds((j % half) * LANES + row, 16)
                            x.append(x_ref[2 * t + j // half, ri, span, :])
                        outs = slab_forward(x, group)
                        for q in range(4):
                            for at in range(2):
                                a, b = two_parts(outs[q][at])
                                span = pl.ds(kind * size + at * LANES + row, 16)
                                eh[q, span, :] = a
                                el[q, span, :] = b
                    x = []
                    for j in range(count):
                        span = pl.ds((j % half) * LANES + row, 16)
                        x.append(h_ref[j // half, span, :])
                    held = slab_forward(x, group)
                    for q in range(4):
                        for at in range(2):
                            eo[q, pl.ds(at * LANES + row, 16), :] = held[q][at]
                    return carry

                lax.fori_loop(0, LANES // 16, rows_of, 0)

        for q in range(4):
            value = dot(wh[q], eh[q]) + dot(wh[q], el[q]) + dot(wl[q], eh[q]) - eo[q]
            slot = pl.program_id(0) * 4 + q
            cos, sin = phase[0, slot], phase[1, slot]
            re, im = value[:LANES], value[LANES:]
            out[q, :LANES, :] = re * cos - im * sin
            out[q, LANES:, :] = re * sin + im * cos

    return pl.pallas_call(
        kernel,
        grid_spec=pltpu.PrefetchScalarGridSpec(
            num_scalar_prefetch=1,
            grid=(GROUPS,),
            in_specs=[whole_block(pieces), whole_block(holos)]
            + [pl.BlockSpec((4, size, kinds * size), lambda g, *_: (g, 0, 0))] * 2,
            out_specs=pl.BlockSpec((4, size, chunk), lambda g, *_: (g, 0, 0)),
            scratch_shapes=[
                pltpu.VMEM((4, kinds * size, chunk), bf16),
                pltpu.VMEM((4, kinds * size, chunk), bf16),
                pltpu.VMEM((4, size, chunk), f32),
            ],
        ),
        out_shape=jax.ShapeDtypeStruct((16, size, chunk), f32),
        compiler_params=params(),
        cost_estimate=pl.CostEstimate(flops=13 * 10**9, bytes_accessed=60 * 10**6, transcendentals=0),
        name="row_forward",
    )(phases, pieces, holos, high, low)


def row_backward(plan, phases, misfit, high, low):
    level, count = plan.level, plan.slab_tiles
    chunk = misfit.shape[-1]
    size = 2 * LANES
    piece = plan.piece

    def kernel(phase, m_ref, wh, wl, out, mh, ml, field):
        kind, step = pl.program_id(0), pl.program_id(1)

        @pl.when(kind == 0)
        def _():
            for q in range(4):
                slot = step * 4 + q
                cos, sin = phase[2, slot], phase[3, slot]
                re, im = m_ref[q, :LANES, :], m_ref[q, LANES:, :]
                for at, value in enumerate((re * cos - im * sin, re * sin + im * cos)):
                    a, b = two_parts(value)
                    mh[slot, at * LANES : (at + 1) * LANES, :] = a
                    ml[slot, at * LANES : (at + 1) * LANES, :] = b

        grads = []
        for q in range(4):
            slot = step * 4 + q
            grads.append(dot(wh[q], mh[slot]) + dot(wh[q], ml[slot]) + dot(wl[q], mh[slot]))
        for group in range(GROUPS):

            @pl.when(step == group)
            def _(group=group):
                for row in range(0, LANES, 16):
                    g = [(v[row : row + 16], v[LANES + row : LANES + row + 16]) for v in grads]
                    values = slab_inverse(g, group, count)
                    for j in range(count):
                        span = pl.ds(j * LANES + row, 16)
                        if group == 0:
                            field[span, :] = values[j]
                        else:
                            field[span, :] = field[span, :] + values[j]

        @pl.when(step == GROUPS - 1)
        def _():
            for s in range(level):
                start = (s % 2) * plan.rows_dev + (s // 2) * piece
                out[s, 0] = field[start : start + piece, :]

    kinds = plan.planes * 2

    return pl.pallas_call(
        kernel,
        grid_spec=pltpu.PrefetchScalarGridSpec(
            num_scalar_prefetch=1,
            grid=(kinds, GROUPS),
            in_specs=[
                pl.BlockSpec((4, size, chunk), lambda kind, step, _: (jnp.where(kind == 0, step, GROUPS - 1), 0, 0)),
                pl.BlockSpec((4, size, size), lambda kind, step, _: (step, 0, kind)),
                pl.BlockSpec((4, size, size), lambda kind, step, _: (step, 0, kind)),
            ],
            out_specs=pl.BlockSpec((level, 1, piece, chunk), lambda kind, step, _: (0, kind, 0, 0)),
            scratch_shapes=[
                pltpu.VMEM((16, size, chunk), bf16),
                pltpu.VMEM((16, size, chunk), bf16),
                pltpu.VMEM((count * LANES, chunk), f32),
            ],
        ),
        out_shape=jax.ShapeDtypeStruct((level, kinds, piece, chunk), f32),
        compiler_params=params(),
        cost_estimate=pl.CostEstimate(flops=13 * 10**9, bytes_accessed=60 * 10**6, transcendentals=0),
        name="row_backward",
    )(phases, misfit, high, low)


def step_pass(plan, pieces, held, tables, transfer):
    rows = min(64, plan.piece)
    level, count = plan.level, len(plan.chunks)
    width = held.shape[-1]
    scale = 1.0 / plan.planes

    def kernel(*refs):
        g_refs, (h_ref, fwd, inv, twd, tra, out), scratch = refs[:count], refs[count : count + 6], refs[count + 6 :]

        def load(tile, row):
            owner, part, at = plan.place_of(tile)
            return (g_refs[part][owner, 0, pl.ds(row, 16), at], g_refs[part][owner, 1, pl.ds(row, 16), at])

        def store(tile, row, value):
            at = slice(tile * LANES, (tile + 1) * LANES)
            for ri in range(2):
                before = h_ref[0, ri, pl.ds(row, 16), at]
                out[0, ri, pl.ds(row, 16), at] = before - scale * value[ri]

        def pick(tile):
            return tra[0, 0, tile : tile + 1, :], tra[0, 1, tile : tile + 1, :]

        lane_convolve(rows, load, store, scratch, fwd, inv, twd, pick)

    fixed = [tables["forward"], tables["inverse"], tables["twiddle"]]
    return pl.pallas_call(
        kernel,
        grid=(plan.planes, plan.piece // rows),
        in_specs=[pl.BlockSpec((level, 2, rows, w), lambda p, i: (0, p, i, 0)) for w in plan.chunks]
        + [pl.BlockSpec((1, 2, rows, width), lambda p, i: (p, 0, i, 0))]
        + [whole_block(a) for a in fixed]
        + [pl.BlockSpec((1, 2, 32, LANES), lambda p, i: (p, 0, 0, 0))],
        out_specs=pl.BlockSpec((1, 2, rows, width), lambda p, i: (p, 0, i, 0)),
        scratch_shapes=lane_scratch(),
        out_shape=jax.ShapeDtypeStruct((plan.planes, 2, plan.piece, width), f32),
        compiler_params=params(),
        cost_estimate=pl.CostEstimate(flops=13 * 10**9, bytes_accessed=51 * 10**6, transcendentals=0),
        name="step_pass",
    )(*pieces, held, *fixed, transfer)


def shrink_pass(plan, scalars, moved, above, below, begin, steps):
    planes, width = plan.planes, moved.shape[-1]
    tiles = plan.piece // 8
    at_top, at_bottom = begin == 0, begin + steps == tiles
    cols = 1024

    def kernel(scal, cur, nxt, up, down, *rest):
        outs, (carry, est) = rest[:planes], rest[planes:]
        i = pl.program_id(0)
        last = jnp.logical_and(i == steps - 1, at_bottom)
        row_ids = lax.broadcasted_iota(jnp.int32, (8, cols), 0)
        lane_ids = lax.broadcasted_iota(jnp.int32, (8, cols), 1)
        end_row = jnp.logical_and(last, scal[1] != 0)

        def flux(tile, next_row, p, start):
            at_end = start + cols == width
            here = [tile(p, ri, start, cols) for ri in range(2)]
            dz, dy, dx = [], [], []
            for ri in range(2):
                if p + 1 < planes:
                    dz.append(tile(p + 1, ri, start, cols) - here[ri])
                follow = jnp.where(row_ids == 7, next_row(p, ri, start), pltpu.roll(here[ri], 7, 0))
                dy.append(follow - here[ri])
                if at_end:
                    ahead = jnp.where(lane_ids == cols - 1, here[ri], pltpu.roll(here[ri], cols - 1, 1))
                else:
                    joined = jnp.concatenate([here[ri], tile(p, ri, start + cols, LANES)], axis=1)
                    ahead = pltpu.roll(joined, cols + LANES - 1, 1)[:, :cols]
                dx.append(ahead - here[ri])
            squares = [v * v for v in dz + dy + dx]
            magnitude = jnp.sqrt(total(squares))
            factor = 1.0 / (1.0 + tv_sharpness * magnitude)
            return here, [v * factor for v in dz], [v * factor for v in dy], [v * factor for v in dx]

        @pl.when(i == 0)
        def _():
            for p in range(planes):
                for start in range(0, width, cols):
                    def tile(p, ri, at, wide):
                        line = slice(0, 1) if at_top else slice(7, 8)
                        return jnp.broadcast_to(up[p, ri, line, at : at + wide], (8, wide))

                    def next_row(p, ri, at):
                        return cur[p, ri, 0:1, at : at + cols]

                    fy = flux(tile, next_row, p, start)[2]
                    for ri in range(2):
                        if at_top:
                            fy[ri] = jnp.where(scal[0] != 0, 0.0, fy[ri])
                        carry[p, ri, :, start : start + cols] = fy[ri]

        def tile(p, ri, at, wide):
            return cur[p, ri, :, at : at + wide]

        def next_row(p, ri, at):
            inner = nxt[p, ri, 0:1, at : at + cols]
            outer = down[p, ri, 0:1, at : at + cols]
            own = cur[p, ri, 7:8, at : at + cols]
            return jnp.where(end_row, own, jnp.where(last, outer, inner))

        prior_x = {}
        for start in range(0, width, cols):
            prior_z = None
            for p in range(planes):
                here, fz, fy, fx = flux(tile, next_row, p, start)
                for ri in range(2):
                    behind_y = jnp.where(row_ids == 0, carry[p, ri, 7:8, start : start + cols], pltpu.roll(fy[ri], 1, 0))
                    if start == 0:
                        behind_x = jnp.where(lane_ids == 0, 0.0, pltpu.roll(fx[ri], 1, 1))
                    else:
                        joined = jnp.concatenate([prior_x[p, ri], fx[ri]], axis=1)
                        behind_x = pltpu.roll(joined, 1, 1)[:, LANES:]
                    divergence = (fy[ri] - behind_y) + (fx[ri] - behind_x)
                    if fz:
                        divergence = divergence + fz[ri]
                    if prior_z:
                        divergence = divergence - prior_z[ri]
                    est[p, ri, :, start : start + cols] = here[ri] + tv_step_size * divergence
                    carry[p, ri, :, start : start + cols] = fy[ri]
                    prior_x[p, ri] = fx[ri][:, cols - LANES :]
                prior_z = fz
        for s in range(planes):
            outs[s][...] = est[jnp.bitwise_xor(scal[2], s)]
    return pl.pallas_call(
        kernel,
        grid_spec=pltpu.PrefetchScalarGridSpec(
            num_scalar_prefetch=1,
            grid=(steps,),
            in_specs=[
                pl.BlockSpec((planes, 2, 8, width), lambda i, _: (0, 0, begin + i, 0)),
                pl.BlockSpec((planes, 2, 8, width), lambda i, _: (0, 0, jnp.minimum(begin + i + 1, tiles - 1), 0)),
                whole_block(above) if at_top else pl.BlockSpec((planes, 2, 8, width), lambda i, _: (0, 0, begin - 1, 0)),
                whole_block(below),
            ],
            out_specs=[pl.BlockSpec((2, 8, width), lambda i, _: (0, i, 0))] * planes,
            scratch_shapes=[
                pltpu.VMEM((planes, 2, 8, width), f32),
                pltpu.VMEM((planes, 2, 8, width), f32),
            ],
        ),
        out_shape=[jax.ShapeDtypeStruct((2, steps * 8, width), f32)] * planes,
        compiler_params=params(),
        cost_estimate=pl.CostEstimate(flops=10**8, bytes_accessed=9 * 10**6, transcendentals=10**6),
        name="shrink_pass",
    )(scalars, moved, moved, above if at_top else moved, below)


def place_rows(plan, scalars, pieces, begin, result):
    rows, width = pieces[0].shape[-2:]
    count = len(pieces)
    given = [] if result is None else [result]

    def kernel(scal, *refs):
        sources, out, sems = refs[:count], refs[count + len(given)], refs[-1]
        ri = pl.program_id(0)
        copies = []
        for s in range(count):
            start = jnp.bitwise_xor(scal[2], s) * plan.piece + begin
            span = pl.ds(pl.multiple_of(start, 8), rows)
            copies.append(pltpu.make_async_copy(sources[s], out.at[pl.ds(ri, 1), span, :], sems.at[s]))
        for copy in copies:
            copy.start()
        for copy in copies:
            copy.wait()

    return pl.pallas_call(
        kernel,
        grid_spec=pltpu.PrefetchScalarGridSpec(
            num_scalar_prefetch=1,
            grid=(2,),
            in_specs=[pl.BlockSpec((1, rows, width), lambda ri, _: (ri, 0, 0))] * count
            + [pl.BlockSpec(memory_space=pl.ANY)] * len(given),
            out_specs=pl.BlockSpec(memory_space=pl.ANY),
            scratch_shapes=[pltpu.SemaphoreType.DMA((count,))],
        ),
        out_shape=jax.ShapeDtypeStruct((2, plan.rows_dev, width), f32),
        input_output_aliases={count + 1: 0} if given else {},
        compiler_params=pltpu.CompilerParams(vmem_limit_bytes=8 * 1024 * 1024),
        cost_estimate=pl.CostEstimate(flops=0, bytes_accessed=9 * 10**6, transcendentals=0),
        name="place_rows",
    )(scalars, *pieces, *given)


class Plan:
    def __init__(self, field_shape, depth, slabs):
        self.planes = depth
        self.slabs = slabs
        self.length = field_shape[-1]
        self.rows_dev = field_shape[-2]
        self.level = depth * 2
        self.cols_dev = self.length // self.level
        tiles = self.cols_dev // LANES
        self.chunks = [LANES] * tiles
        self.starts = [sum(self.chunks[:i]) for i in range(len(self.chunks))]
        self.piece = self.rows_dev // depth
        self.slab_tiles = 2 * self.rows_dev // LANES

    def place_of(self, tile):
        owner, inner = divmod(tile * LANES, self.cols_dev)
        part = max(i for i, start in enumerate(self.starts) if start <= inner)
        first = inner - self.starts[part]
        return owner, part, slice(first, first + LANES)


def swapped(value, axes, size, step):
    return lax.ppermute(value, axes, [(i, i ^ step) for i in range(size)])


def after(value, *others):
    return lax.optimization_barrier((value,) + others)[0]


def halving_steps(size):
    steps = []
    step = 1
    while step < size:
        steps.append(step)
        step = step * 2
    return steps


def scatter_step(value, axis, size, position, step, others):
    upper = jnp.bitwise_and(position, step) != 0
    half = value.shape[0] // 2
    kept = jnp.where(upper, value[half:], value[:half])
    given = jnp.where(upper, value[:half], value[half:])
    return kept + swapped(after(given, *others), axis, size, step)


def gather_step(value, axis, size, position, step, others):
    upper = jnp.bitwise_and(position, step) != 0
    other = swapped(after(value, *others), axis, size, step)
    return jnp.concatenate([jnp.where(upper, other, value), jnp.where(upper, value, other)])


def exchanged(value, axes):
    return lax.all_to_all(value, axes, 0, 0, tiled=True)


def per_device(field, hologram, defocus):
    depth, slabs = lax.axis_size("depth"), lax.axis_size("slab")
    plan = Plan(field.shape, depth, slabs)
    length = plan.length
    d, z, c = lax.axis_index("depth"), lax.axis_index("slab"), lax.axis_index("core")
    me = d * 2 + c
    order = (z * 2 + c) * depth + d
    n_order = slabs * 2 * depth
    ends = jnp.stack([(order == 0).astype(jnp.int32), (order == n_order - 1).astype(jnp.int32), d.astype(jnp.int32)])
    level_axes = ("depth", "core")

    forward, inverse = lane_tables()
    tables = {
        "forward": jnp.asarray(forward),
        "inverse": jnp.asarray(inverse),
        "twiddle": jnp.asarray(twiddle_table(length, 32)),
    }
    column_freqs = np.arange(32)[:, None] + 32 * np.arange(LANES)[None, :]
    cos, sin = chirp(defocus[0], column_freqs, length)
    transfer = jnp.stack([cos, -sin]) * (1.0 / length)

    ordered = jnp.concatenate([defocus] + [swapped(defocus, "depth", depth, s) for s in range(1, depth)])
    depths = ordered[jnp.bitwise_xor(jnp.arange(depth, dtype=jnp.int32), d)]

    own = field[:, 0]
    quarters = max(1, min(4, plan.piece // 8))
    early = cut_rows(plan, own, 0, quarters)
    own, early = lax.optimization_barrier((own, early))
    early, depths = lax.optimization_barrier((early, depths))
    held = [exchanged(early, "depth")]

    sent = column_pass(plan, own, tables, transfer)
    bases, freqs = slot_bases(length)
    cos, sin = chirp(depths[None, :, None], freqs[:, None, :], length)
    weights = jnp.stack([cos, sin], axis=2).reshape(16, 2 * depth, 2 * LANES)
    weights, bases, *sent = lax.optimization_barrier((weights, jnp.asarray(bases), *sent))
    high, low = slot_matrices(plan, bases, weights)

    slot_k = np.array([g + 4 * q for g in range(GROUPS) for q in range(4)])
    turns = (jnp.asarray(slot_k * plan.slab_tiles, jnp.int32) * z) % 32
    angle = turns.astype(f32) * (2.0 * math.pi / 32)
    unit = jnp.asarray(np.where(slot_k == 0, 1.0 / 32, 2.0 / 32), f32)
    phases = jnp.stack([jnp.cos(angle), -jnp.sin(angle), jnp.cos(angle) * unit, jnp.sin(angle) * unit])

    mine = lax.dynamic_slice_in_dim(hologram, me * plan.cols_dev, plan.cols_dev, 1)
    theirs = lax.dynamic_slice_in_dim(hologram, jnp.bitwise_xor(me, 1) * plan.cols_dev, plan.cols_dev, 1)
    theirs = swapped(theirs, "core", 2, 1)
    holos = jnp.where(c == 0, jnp.stack([mine, theirs]), jnp.stack([theirs, mine]))

    count = len(plan.chunks)

    def forward_stage(value, part, others):
        start = plan.starts[part]
        here = holos[:, :, start : start + plan.chunks[part]]
        return row_forward(plan, phases, after(value, *others), here, high, low)

    def backward_stage(value, part, others):
        return row_backward(plan, phases, after(value, *others), high, low)

    def sum_stage(function, step):
        return lambda value, part, others: function(value, "slab", slabs, z, step, others)

    halvings = halving_steps(slabs)
    stages = [forward_stage]
    stages += [sum_stage(scatter_step, step) for step in halvings]
    stages += [sum_stage(gather_step, step) for step in reversed(halvings)]
    stages += [backward_stage]

    queue = list(sent) + [None] * (quarters - 1)
    state = [None] * count
    before, back = [held[0]], []
    slot = 0
    while len(back) < count:
        others, before = before, []
        if queue:
            value = queue.pop(0)
            if value is None:
                value = cut_rows(plan, field[:, 0], len(held), quarters)
                held.append(exchanged(after(value, *others), "depth"))
                before.append(held[-1])
            else:
                before.append(exchanged(after(value, *others), level_axes))
                if slot < count:
                    state[slot] = before[-1]
                else:
                    back.append(before[-1])
        for part in range(count):
            number = slot - (part + 1)
            if 0 <= number < len(stages):
                state[part] = stages[number](state[part], part, others)
                before.append(state[part])
                if number == len(stages) - 1:
                    queue.append(state[part])
        if slot == 0:
            before += [high, low]
        slot += 1

    held = jnp.stack(held, axis=2).reshape(depth, 2, plan.piece, length)
    cos, sin = chirp(depths[:, None, None], column_freqs[None], length)
    transfer = jnp.stack([cos, sin], axis=1) * (1.0 / length)
    moved = step_pass(plan, back, held, tables, transfer)

    all_axes = ("depth", "slab", "core")
    device_at = [(i % depth) * (slabs * 2) + i // depth for i in range(n_order)]
    downward = [(device_at[i], device_at[i + 1]) for i in range(n_order - 1)]
    above = lax.ppermute(moved[:, :, -1:], all_axes, downward)
    below = lax.ppermute(moved[:, :, :1], all_axes, [(b, a) for a, b in downward])
    tiles = plan.piece // 8
    steps = max(1, tiles // 4)
    result = None
    for begin in range(0, tiles, steps):
        parts = shrink_pass(plan, ends, moved, above, below, begin, steps)
        parts = [parts[0]] + [swapped(parts[s], "depth", depth, s) for s in range(1, depth)]
        result = place_rows(plan, ends, parts, begin * 8, result)
    return result.reshape(field.shape)


def solution(mesh):
    depth, row = mesh.shape["depth"], mesh.shape["row"]
    split = Mesh(mesh.devices.reshape(depth, row // 2, 2), ("depth", "slab", "core"))
    rows = ("slab", "core")
    return jax.shard_map(
        per_device,
        mesh=split,
        in_specs=(P(None, "depth", rows, None), P(rows, None), P("depth")),
        out_specs=P(None, "depth", rows, None),
        check_vma=False,
    )
```

```python
import math

import jax
import jax.numpy as jnp
import numpy as np
from jax import lax
from jax.experimental import pallas as pl
from jax.experimental.pallas import tpu as pltpu
from jax.sharding import Mesh, PartitionSpec as P

tv_step_size = 1.0 / 12.0
tv_sharpness = 0.25
LANES = 128
GROUPS = 4
VMEM_BYTES = 60 * 1024 * 1024
f32 = jnp.float32
bf16 = jnp.bfloat16


def c_add(u, v):
    return (u[0] + v[0], u[1] + v[1])


def c_sub(u, v):
    return (u[0] - v[0], u[1] - v[1])


def c_rot(u, num, den):
    num = num % den
    if num == 0:
        return u
    if 4 * num == den:
        return (-u[1], u[0])
    if 2 * num == den:
        return (-u[0], -u[1])
    if 4 * num == 3 * den:
        return (u[1], -u[0])
    if (8 * num) % den == 0:
        half = math.sqrt(0.5)
        eighth = (8 * num) // den
        plus = (u[0] + u[1]) * half
        minus = (u[0] - u[1]) * half
        if eighth == 1:
            return (minus, plus)
        if eighth == 3:
            return (-plus, minus)
        if eighth == 5:
            return (-minus, -plus)
        return (plus, -minus)
    cos = math.cos(2 * math.pi * num / den)
    sin = math.sin(2 * math.pi * num / den)
    return (u[0] * cos - u[1] * sin, u[0] * sin + u[1] * cos)


def dft4(v, sign):
    s, d = c_add(v[0], v[2]), c_sub(v[0], v[2])
    t, u = c_add(v[1], v[3]), c_sub(v[1], v[3])
    u = c_rot(u, sign, 4)
    return [c_add(s, t), c_add(d, u), c_sub(s, t), c_sub(d, u)]


def dft8(v, sign):
    even, odd = dft4(v[0::2], sign), dft4(v[1::2], sign)
    odd = [c_rot(odd[q], sign * q, 8) for q in range(4)]
    return [c_add(even[q], odd[q]) for q in range(4)] + [c_sub(even[q], odd[q]) for q in range(4)]


def real_rot(value, num, den):
    cos = math.cos(2 * math.pi * num / den)
    sin = math.sin(2 * math.pi * num / den)
    return (value * cos, value * sin)


def total(values):
    out = values[0]
    for value in values[1:]:
        out = out + value
    return out


def slab_forward(x, group):
    count = len(x)
    if group == 0 and count == 8:
        s0, d0, s1, d1 = x[0] + x[4], x[0] - x[4], x[2] + x[6], x[2] - x[6]
        s2, d2, s3, d3 = x[1] + x[5], x[1] - x[5], x[3] + x[7], x[3] - x[7]
        e0, e2, o0, o2 = s0 + s1, s0 - s1, s2 + s3, s2 - s3
        p1 = c_rot((d2, -d3), -1, 8)
        p3 = c_rot((d2, d3), -3, 8)
        return [(e0 + o0, e0 - o0), (d0 + p1[0], p1[1] - d1), (e2, -o2), (d0 + p3[0], d1 + p3[1])]
    if count == 8:
        w = [(x[0], None)] + [real_rot(x[j], -group * j, 32) for j in range(1, 8)]
        s, d = (x[0] + w[4][0], w[4][1]), (x[0] - w[4][0], -w[4][1])
        t, u = c_add(w[2], w[6]), c_rot(c_sub(w[2], w[6]), -1, 4)
        even = [c_add(s, t), c_add(d, u), c_sub(s, t), c_sub(d, u)]
        odd = dft4(w[1::2], -1)
        return [c_add(even[q], c_rot(odd[q], -q, 8)) for q in range(4)]
    outs = []
    for q in range(4):
        parts = [real_rot(x[j], -(group + 4 * q) * j, 32) for j in range(count)]
        outs.append((total([v[0] for v in parts]), total([v[1] for v in parts])))
    if group == 0:
        outs[0] = (total(x), total([x[j] if j % 2 == 0 else -x[j] for j in range(count)]))
    return outs


def slab_inverse(g, group, count):
    if group == 0:
        (top, alt), rest = g[0], g[1:]
        if count == 8:
            (a1, b1), (a2, b2), (a3, b3) = rest
            half = math.sqrt(0.5)
            p, m = top + alt, top - alt
            s13, d13 = a1 + a3, b1 - b3
            x0, x4 = p + a2 + s13, p + a2 - s13
            x2, x6 = p - a2 - d13, p - a2 + d13
            u = (a1 - a3) * half
            v = (b1 + b3) * half
            x1, x5 = m - b2 + (u - v), m - b2 - (u - v)
            x3, x7 = m + b2 - (u + v), m + b2 + (u + v)
            return [x0, x1, x2, x3, x4, x5, x6, x7]
        outs = []
        for j in range(count):
            terms = [c_rot(rest[q - 1], q * j, 8)[0] for q in range(1, 4)]
            outs.append((top + alt if j % 2 == 0 else top - alt) + total(terms))
        return outs
    if count == 8:
        even = dft4(g, 1)
        odd = dft4([c_rot(g[q], q, 8) for q in range(4)], 1)
        v = [even[0], odd[0], even[1], odd[1], even[2], odd[2], even[3], odd[3]]
        outs = [v[0][0]]
        for j in range(1, 8):
            cos = math.cos(2 * math.pi * group * j / 32)
            sin = math.sin(2 * math.pi * group * j / 32)
            outs.append(v[j][0] * cos - v[j][1] * sin)
        return outs
    outs = []
    for j in range(count):
        terms = [c_rot(g[q], (group + 4 * q) * j, 32)[0] for q in range(4)]
        outs.append(total(terms))
    return outs


def two_parts(value):
    high = value.astype(bf16)
    low = (value - high.astype(f32)).astype(bf16)
    return high, low


def dot(left, right):
    return jnp.dot(left, right, preferred_element_type=f32)


def host_parts(matrix):
    high = matrix.astype(np.float32).astype(jnp.bfloat16)
    low = (matrix - high.astype(np.float64)).astype(np.float32).astype(jnp.bfloat16)
    return high, low


def lane_tables():
    n = np.arange(LANES)
    angle = 2 * np.pi * (n[:, None] * n[None, :] % LANES) / LANES
    cos, sin = np.cos(angle), np.sin(angle)
    forward = np.block([[cos, -sin], [sin, cos]])
    inverse = np.block([[cos, sin], [-sin, cos]])
    stacked = []
    for matrix in (forward, inverse):
        high, low = host_parts(matrix)
        stacked.append(np.concatenate([high, high, low], axis=0))
    return stacked


def twiddle_table(length, tiles):
    k = np.arange(tiles)[:, None]
    n = np.arange(LANES)[None, :]
    angle = -2 * np.pi * (k * n % length) / length
    return np.stack([np.cos(angle), np.sin(angle)]).astype(np.float32)


def slot_bases(length):
    n = np.arange(LANES)[:, None]
    bases = np.zeros((16, 2 * LANES, 2 * LANES))
    freqs = np.zeros((16, 2 * LANES), np.int64)
    for group in range(GROUPS):
        for q in range(4):
            k = group + 4 * q
            slot = group * 4 + q
            if k == 0:
                column = 0
                for half, start in ((0, 0), (1, 16)):
                    rows = slice(half * LANES, (half + 1) * LANES)
                    for step in range(LANES // 2 + 1):
                        a = start + 32 * step
                        if a > length // 2:
                            continue
                        angle = 2 * np.pi * (a * n[:, 0] % length) / length
                        if a in (0, length // 2):
                            bases[slot, rows, column] = np.cos(angle) / np.sqrt(LANES)
                            freqs[slot, column] = a
                            column += 1
                            continue
                        bases[slot, rows, column] = np.cos(angle) * np.sqrt(2 / LANES)
                        bases[slot, rows, column + 1] = np.sin(angle) * np.sqrt(2 / LANES)
                        freqs[slot, column : column + 2] = a
                        column += 2
                assert column == 2 * LANES
                continue
            a = k + 32 * np.arange(LANES)[None, :]
            angle = 2 * np.pi * (a * n % length) / length
            cos, sin = np.cos(angle) / np.sqrt(LANES), np.sin(angle) / np.sqrt(LANES)
            bases[slot] = np.block([[cos, -sin], [sin, cos]])
            freqs[slot] = np.concatenate([a[0], a[0]])
    return bases.astype(np.float32), freqs


def chirp(depth_values, freqs, length):
    centred = np.where(freqs < length // 2, freqs, freqs - length)
    squares = (centred.astype(np.int64) ** 2).astype(np.int64)
    coarse = (squares // 2048 * 2048).astype(np.float32)
    fine = (squares % 2048).astype(np.float32)
    unit = 0.5 / (float(length) * float(length))
    whole = jnp.floor(depth_values * 2.0) * 0.5
    rest = depth_values - whole

    def turn(left, right):
        value = left * right * unit
        return value - jnp.floor(value)

    turns = turn(whole, coarse) + turn(whole, fine) + rest * (coarse * unit) + rest * (fine * unit)
    angle = (turns - jnp.floor(turns)) * (2.0 * math.pi)
    return jnp.cos(angle), jnp.sin(angle)


def lane_convolve(rows, load, store, scratch, forward_ref, inverse_ref, twiddle_ref, transfer):
    ahead, behind = scratch[0], scratch[1]
    parts, spec = scratch[2:4], scratch[4:6]

    def twiddle(tile):
        return twiddle_ref[0, tile : tile + 1, :], twiddle_ref[1, tile : tile + 1, :]

    def forward(chunk):
        row, out = chunk * 16, parts[chunk % 2]
        for b in range(8):
            x = [load(8 * a + b, row) for a in range(4)]
            y = dft4(x, -1)
            for k in range(4):
                v = c_rot(y[k], -b * k, 32)
                ahead[0, k * 8 + b] = v[0]
                ahead[1, k * 8 + b] = v[1]
        for k in range(4):
            y = dft8([(ahead[0, k * 8 + b], ahead[1, k * 8 + b]) for b in range(8)], -1)
            for m in range(8):
                tile = k + 4 * m
                tr, ti = twiddle(tile)
                re, im = y[m]
                span = slice(tile * 16, tile * 16 + 16)
                for at, value in enumerate((re * tr - im * ti, re * ti + im * tr)):
                    high, low = two_parts(value)
                    out[span, at * LANES : (at + 1) * LANES] = high
                    out[span, (2 + at) * LANES : (3 + at) * LANES] = low
                    out[span, (4 + at) * LANES : (5 + at) * LANES] = high

    def middle(chunk):
        taken, out = parts[chunk % 2], spec[chunk % 2]
        for first in range(0, 32, 16):
            span = slice(first * 16, first * 16 + 256)
            value = dot(taken[span, :], forward_ref[...])
            pieces = []
            for t in range(16):
                tr, ti = transfer(first + t)
                re, im = value[t * 16 : t * 16 + 16, :LANES], value[t * 16 : t * 16 + 16, LANES:]
                pieces.append(jnp.concatenate([re * tr - im * ti, re * ti + im * tr], axis=1))
            high, low = two_parts(jnp.concatenate(pieces, axis=0))
            out[span, :] = dot(jnp.concatenate([high, low, high], axis=1), inverse_ref[...])

    def inverse(chunk):
        row, taken = chunk * 16, spec[chunk % 2]
        for k in range(4):
            x = []
            for m in range(8):
                tile = k + 4 * m
                tr, ti = twiddle(tile)
                span = slice(tile * 16, tile * 16 + 16)
                re, im = taken[span, :LANES], taken[span, LANES:]
                x.append((re * tr + im * ti, im * tr - re * ti))
            y = dft8(x, 1)
            for b in range(8):
                v = c_rot(y[b], b * k, 32)
                behind[0, k * 8 + b] = v[0]
                behind[1, k * 8 + b] = v[1]
        for b in range(8):
            y = dft4([(behind[0, k * 8 + b], behind[1, k * 8 + b]) for k in range(4)], 1)
            for a in range(4):
                store(8 * a + b, row, y[a])

    count = rows // 16
    for t in range(count + 2):
        if t < count:
            forward(t)
        if 0 <= t - 1 < count:
            middle(t - 1)
        if 0 <= t - 2 < count:
            inverse(t - 2)


def lane_scratch():
    work = pltpu.VMEM((2, 32, 16, LANES), f32)
    parts = pltpu.VMEM((512, 6 * LANES), bf16)
    spec = pltpu.VMEM((512, 2 * LANES), f32)
    return [work, work, parts, parts, spec, spec]


def params():
    return pltpu.CompilerParams(vmem_limit_bytes=VMEM_BYTES)


def whole_block(array):
    rank = array.ndim
    return pl.BlockSpec(array.shape, lambda *_: (0,) * rank)


def column_pass(plan, field, tables, transfer):
    rows = min(64, plan.rows_dev)
    level, count = plan.level, len(plan.chunks)

    def kernel(f_ref, fwd, inv, twd, tra, *rest):
        outs, scratch = rest[:count], rest[count:]

        def load(tile, row):
            at = slice(tile * LANES, (tile + 1) * LANES)
            return (f_ref[0, pl.ds(row, 16), at], f_ref[1, pl.ds(row, 16), at])

        def store(tile, row, value):
            owner, part, at = plan.place_of(tile)
            outs[part][owner, 0, pl.ds(row, 16), at] = value[0]
            outs[part][owner, 1, pl.ds(row, 16), at] = value[1]

        def pick(tile):
            return tra[0, tile : tile + 1, :], tra[1, tile : tile + 1, :]

        lane_convolve(rows, load, store, scratch, fwd, inv, twd, pick)

    width = field.shape[-1]
    fixed = [tables["forward"], tables["inverse"], tables["twiddle"], transfer]
    return pl.pallas_call(
        kernel,
        grid=(plan.rows_dev // rows,),
        in_specs=[pl.BlockSpec((2, rows, width), lambda i: (0, i, 0))] + [whole_block(a) for a in fixed],
        out_specs=[pl.BlockSpec((level, 2, rows, w), lambda i: (0, 0, i, 0)) for w in plan.chunks],
        scratch_shapes=lane_scratch(),
        out_shape=[jax.ShapeDtypeStruct((level, 2, plan.rows_dev, w), f32) for w in plan.chunks],
        compiler_params=params(),
        cost_estimate=pl.CostEstimate(flops=13 * 10**9, bytes_accessed=34 * 10**6, transcendentals=0),
        name="column_pass",
    )(field, *fixed)


def cut_rows(plan, field, first, count):
    width = field.shape[-1]
    rows, units = plan.piece // plan.units, plan.units

    def kernel(x_ref, out_ref):
        out_ref[0] = x_ref[...]

    return pl.pallas_call(
        kernel,
        grid=(plan.planes, count),
        in_specs=[pl.BlockSpec((2, rows, width), lambda p, u: (0, p * units + first + u, 0))],
        out_specs=pl.BlockSpec((1, 2, rows, width), lambda p, u: (p, 0, u, 0)),
        out_shape=jax.ShapeDtypeStruct((plan.planes, 2, rows * count, width), f32),
        compiler_params=params(),
        cost_estimate=pl.CostEstimate(flops=0, bytes_accessed=9 * 10**6, transcendentals=0),
        name="cut_rows",
    )(field)


def slot_matrices(plan, bases, weights):
    kinds = weights.shape[1]
    size = 2 * LANES

    def kernel(b_ref, w_ref, high_ref, low_ref):
        basis = b_ref[0]
        for kind in range(kinds):
            scaled = basis * w_ref[0, kind : kind + 1, :]
            product = lax.dot_general(
                scaled,
                basis,
                (((1,), (1,)), ((), ())),
                precision=lax.Precision.HIGHEST,
                preferred_element_type=f32,
            )
            high, low = two_parts(product)
            high_ref[0, :, kind * size : (kind + 1) * size] = high
            low_ref[0, :, kind * size : (kind + 1) * size] = low

    shape = jax.ShapeDtypeStruct((16, size, kinds * size), bf16)
    return pl.pallas_call(
        kernel,
        grid=(16,),
        in_specs=[
            pl.BlockSpec((1, size, size), lambda i: (i, 0, 0)),
            pl.BlockSpec((1, kinds, size), lambda i: (i, 0, 0)),
        ],
        out_specs=[pl.BlockSpec((1, size, kinds * size), lambda i: (i, 0, 0))] * 2,
        out_shape=[shape, shape],
        compiler_params=params(),
        cost_estimate=pl.CostEstimate(flops=26 * 10**9, bytes_accessed=34 * 10**6, transcendentals=0),
        name="slot_matrices",
    )(bases, weights)


def row_forward(plan, phases, pieces, holos, high, low):
    count = plan.slab_tiles
    chunk = pieces.shape[-1]
    kinds = plan.planes * 2
    size = 2 * LANES
    half = count // 2

    def kernel(phase, x_ref, h_ref, wh, wl, out, eh, el, eo):
        for group in range(GROUPS):

            @pl.when(pl.program_id(0) == group)
            def _(group=group):
                def rows_of(i, carry):
                    row = i * 16
                    for kind in range(kinds):
                        t, ri = kind // 2, kind % 2

                        x = []
                        for j in range(count):
                            span = pl.ds((j % half) * LANES + row, 16)
                            x.append(x_ref[2 * t + j // half, ri, span, :])
                        outs = slab_forward(x, group)
                        for q in range(4):
                            for at in range(2):
                                a, b = two_parts(outs[q][at])
                                span = pl.ds(kind * size + at * LANES + row, 16)
                                eh[q, span, :] = a
                                el[q, span, :] = b
                    x = []
                    for j in range(count):
                        span = pl.ds((j % half) * LANES + row, 16)
                        x.append(h_ref[j // half, span, :])
                    held = slab_forward(x, group)
                    for q in range(4):
                        for at in range(2):
                            eo[q, pl.ds(at * LANES + row, 16), :] = held[q][at]
                    return carry

                lax.fori_loop(0, LANES // 16, rows_of, 0)

        for q in range(4):
            value = dot(wh[q], eh[q]) + dot(wh[q], el[q]) + dot(wl[q], eh[q]) - eo[q]
            slot = pl.program_id(0) * 4 + q
            cos, sin = phase[0, slot], phase[1, slot]
            re, im = value[:LANES], value[LANES:]
            out[q, :LANES, :] = re * cos - im * sin
            out[q, LANES:, :] = re * sin + im * cos

    return pl.pallas_call(
        kernel,
        grid_spec=pltpu.PrefetchScalarGridSpec(
            num_scalar_prefetch=1,
            grid=(GROUPS,),
            in_specs=[whole_block(pieces), whole_block(holos)]
            + [pl.BlockSpec((4, size, kinds * size), lambda g, *_: (g, 0, 0))] * 2,
            out_specs=pl.BlockSpec((4, size, chunk), lambda g, *_: (g, 0, 0)),
            scratch_shapes=[
                pltpu.VMEM((4, kinds * size, chunk), bf16),
                pltpu.VMEM((4, kinds * size, chunk), bf16),
                pltpu.VMEM((4, size, chunk), f32),
            ],
        ),
        out_shape=jax.ShapeDtypeStruct((16, size, chunk), f32),
        compiler_params=params(),
        cost_estimate=pl.CostEstimate(flops=13 * 10**9, bytes_accessed=60 * 10**6, transcendentals=0),
        name="row_forward",
    )(phases, pieces, holos, high, low)


def row_backward(plan, phases, misfit, high, low):
    level, count = plan.level, plan.slab_tiles
    chunk = misfit.shape[-1]
    size = 2 * LANES
    piece = plan.piece

    def kernel(phase, m_ref, wh, wl, out, mh, ml, field):
        kind, step = pl.program_id(0), pl.program_id(1)

        @pl.when(kind == 0)
        def _():
            for q in range(4):
                slot = step * 4 + q
                cos, sin = phase[2, slot], phase[3, slot]
                re, im = m_ref[q, :LANES, :], m_ref[q, LANES:, :]
                for at, value in enumerate((re * cos - im * sin, re * sin + im * cos)):
                    a, b = two_parts(value)
                    mh[slot, at * LANES : (at + 1) * LANES, :] = a
                    ml[slot, at * LANES : (at + 1) * LANES, :] = b

        grads = []
        for q in range(4):
            slot = step * 4 + q
            grads.append(dot(wh[q], mh[slot]) + dot(wh[q], ml[slot]) + dot(wl[q], mh[slot]))
        for group in range(GROUPS):

            @pl.when(step == group)
            def _(group=group):
                for row in range(0, LANES, 16):
                    g = [(v[row : row + 16], v[LANES + row : LANES + row + 16]) for v in grads]
                    values = slab_inverse(g, group, count)
                    for j in range(count):
                        span = pl.ds(j * LANES + row, 16)
                        if group == 0:
                            field[span, :] = values[j]
                        else:
                            field[span, :] = field[span, :] + values[j]

        @pl.when(step == GROUPS - 1)
        def _():
            for s in range(level):
                start = (s % 2) * plan.rows_dev + (s // 2) * piece
                out[s, 0] = field[start : start + piece, :]

    kinds = plan.planes * 2

    return pl.pallas_call(
        kernel,
        grid_spec=pltpu.PrefetchScalarGridSpec(
            num_scalar_prefetch=1,
            grid=(kinds, GROUPS),
            in_specs=[
                pl.BlockSpec((4, size, chunk), lambda kind, step, _: (jnp.where(kind == 0, step, GROUPS - 1), 0, 0)),
                pl.BlockSpec((4, size, size), lambda kind, step, _: (step, 0, kind)),
                pl.BlockSpec((4, size, size), lambda kind, step, _: (step, 0, kind)),
            ],
            out_specs=pl.BlockSpec((level, 1, piece, chunk), lambda kind, step, _: (0, kind, 0, 0)),
            scratch_shapes=[
                pltpu.VMEM((16, size, chunk), bf16),
                pltpu.VMEM((16, size, chunk), bf16),
                pltpu.VMEM((count * LANES, chunk), f32),
            ],
        ),
        out_shape=jax.ShapeDtypeStruct((level, kinds, piece, chunk), f32),
        compiler_params=params(),
        cost_estimate=pl.CostEstimate(flops=13 * 10**9, bytes_accessed=60 * 10**6, transcendentals=0),
        name="row_backward",
    )(phases, misfit, high, low)


def step_pass(plan, pieces, held, tables, transfer):
    rows = min(64, plan.piece)
    level, count = plan.level, len(plan.chunks)
    width = held.shape[-1]
    scale = 1.0 / plan.planes

    def kernel(*refs):
        g_refs, (h_ref, fwd, inv, twd, tra, out), scratch = refs[:count], refs[count : count + 6], refs[count + 6 :]

        def load(tile, row):
            owner, part, at = plan.place_of(tile)
            return (g_refs[part][owner, 0, pl.ds(row, 16), at], g_refs[part][owner, 1, pl.ds(row, 16), at])

        def store(tile, row, value):
            at = slice(tile * LANES, (tile + 1) * LANES)
            for ri in range(2):
                before = h_ref[0, ri, pl.ds(row, 16), at]
                out[0, ri, pl.ds(row, 16), at] = before - scale * value[ri]

        def pick(tile):
            return tra[0, 0, tile : tile + 1, :], tra[0, 1, tile : tile + 1, :]

        lane_convolve(rows, load, store, scratch, fwd, inv, twd, pick)

    fixed = [tables["forward"], tables["inverse"], tables["twiddle"]]
    return pl.pallas_call(
        kernel,
        grid=(plan.planes, plan.piece // rows),
        in_specs=[pl.BlockSpec((level, 2, rows, w), lambda p, i: (0, p, i, 0)) for w in plan.chunks]
        + [pl.BlockSpec((1, 2, rows, width), lambda p, i: (p, 0, i, 0))]
        + [whole_block(a) for a in fixed]
        + [pl.BlockSpec((1, 2, 32, LANES), lambda p, i: (p, 0, 0, 0))],
        out_specs=pl.BlockSpec((1, 2, rows, width), lambda p, i: (p, 0, i, 0)),
        scratch_shapes=lane_scratch(),
        out_shape=jax.ShapeDtypeStruct((plan.planes, 2, plan.piece, width), f32),
        compiler_params=params(),
        cost_estimate=pl.CostEstimate(flops=13 * 10**9, bytes_accessed=51 * 10**6, transcendentals=0),
        name="step_pass",
    )(*pieces, held, *fixed, transfer)


def shrink_pass(plan, scalars, moved, above, below, begin, steps):
    planes, width = plan.planes, moved.shape[-1]
    tiles = plan.piece // 8
    at_top, at_bottom = begin == 0, begin + steps == tiles
    cols = 1024

    def kernel(scal, cur, nxt, up, down, *rest):
        outs, (carry, est) = rest[:planes], rest[planes:]
        i = pl.program_id(0)
        last = jnp.logical_and(i == steps - 1, at_bottom)
        row_ids = lax.broadcasted_iota(jnp.int32, (8, cols), 0)
        lane_ids = lax.broadcasted_iota(jnp.int32, (8, cols), 1)
        end_row = jnp.logical_and(last, scal[1] != 0)

        def flux(tile, next_row, p, start):
            at_end = start + cols == width
            here = [tile(p, ri, start, cols) for ri in range(2)]
            dz, dy, dx = [], [], []
            for ri in range(2):
                if p + 1 < planes:
                    dz.append(tile(p + 1, ri, start, cols) - here[ri])
                follow = jnp.where(row_ids == 7, next_row(p, ri, start), pltpu.roll(here[ri], 7, 0))
                dy.append(follow - here[ri])
                if at_end:
                    ahead = jnp.where(lane_ids == cols - 1, here[ri], pltpu.roll(here[ri], cols - 1, 1))
                else:
                    joined = jnp.concatenate([here[ri], tile(p, ri, start + cols, LANES)], axis=1)
                    ahead = pltpu.roll(joined, cols + LANES - 1, 1)[:, :cols]
                dx.append(ahead - here[ri])
            squares = [v * v for v in dz + dy + dx]
            magnitude = jnp.sqrt(total(squares))
            factor = 1.0 / (1.0 + tv_sharpness * magnitude)
            return here, [v * factor for v in dz], [v * factor for v in dy], [v * factor for v in dx]

        @pl.when(i == 0)
        def _():
            for p in range(planes):
                for start in range(0, width, cols):
                    def tile(p, ri, at, wide):
                        line = slice(0, 1) if at_top else slice(7, 8)
                        return jnp.broadcast_to(up[p, ri, line, at : at + wide], (8, wide))

                    def next_row(p, ri, at):
                        return cur[p, ri, 0:1, at : at + cols]

                    fy = flux(tile, next_row, p, start)[2]
                    for ri in range(2):
                        if at_top:
                            fy[ri] = jnp.where(scal[0] != 0, 0.0, fy[ri])
                        carry[p, ri, :, start : start + cols] = fy[ri]

        def tile(p, ri, at, wide):
            return cur[p, ri, :, at : at + wide]

        def next_row(p, ri, at):
            inner = nxt[p, ri, 0:1, at : at + cols]
            outer = down[p, ri, 0:1, at : at + cols]
            own = cur[p, ri, 7:8, at : at + cols]
            return jnp.where(end_row, own, jnp.where(last, outer, inner))

        prior_x = {}
        for start in range(0, width, cols):
            prior_z = None
            for p in range(planes):
                here, fz, fy, fx = flux(tile, next_row, p, start)
                for ri in range(2):
                    behind_y = jnp.where(row_ids == 0, carry[p, ri, 7:8, start : start + cols], pltpu.roll(fy[ri], 1, 0))
                    if start == 0:
                        behind_x = jnp.where(lane_ids == 0, 0.0, pltpu.roll(fx[ri], 1, 1))
                    else:
                        joined = jnp.concatenate([prior_x[p, ri], fx[ri]], axis=1)
                        behind_x = pltpu.roll(joined, 1, 1)[:, LANES:]
                    divergence = (fy[ri] - behind_y) + (fx[ri] - behind_x)
                    if fz:
                        divergence = divergence + fz[ri]
                    if prior_z:
                        divergence = divergence - prior_z[ri]
                    est[p, ri, :, start : start + cols] = here[ri] + tv_step_size * divergence
                    carry[p, ri, :, start : start + cols] = fy[ri]
                    prior_x[p, ri] = fx[ri][:, cols - LANES :]
                prior_z = fz
        for s in range(planes):
            outs[s][...] = est[jnp.bitwise_xor(scal[2], s)]
    return pl.pallas_call(
        kernel,
        grid_spec=pltpu.PrefetchScalarGridSpec(
            num_scalar_prefetch=1,
            grid=(steps,),
            in_specs=[
                pl.BlockSpec((planes, 2, 8, width), lambda i, _: (0, 0, begin + i, 0)),
                pl.BlockSpec((planes, 2, 8, width), lambda i, _: (0, 0, jnp.minimum(begin + i + 1, tiles - 1), 0)),
                whole_block(above) if at_top else pl.BlockSpec((planes, 2, 8, width), lambda i, _: (0, 0, begin - 1, 0)),
                whole_block(below),
            ],
            out_specs=[pl.BlockSpec((2, 8, width), lambda i, _: (0, i, 0))] * planes,
            scratch_shapes=[
                pltpu.VMEM((planes, 2, 8, width), f32),
                pltpu.VMEM((planes, 2, 8, width), f32),
            ],
        ),
        out_shape=[jax.ShapeDtypeStruct((2, steps * 8, width), f32)] * planes,
        compiler_params=params(),
        cost_estimate=pl.CostEstimate(flops=10**8, bytes_accessed=9 * 10**6, transcendentals=10**6),
        name="shrink_pass",
    )(scalars, moved, moved, above if at_top else moved, below)


def place_rows(plan, scalars, pieces, begin, result):
    rows, width = pieces[0].shape[-2:]
    count = len(pieces)
    given = [] if result is None else [result]

    def kernel(scal, *refs):
        sources, out, sems = refs[:count], refs[count + len(given)], refs[-1]
        ri = pl.program_id(0)
        copies = []
        for s in range(count):
            start = jnp.bitwise_xor(scal[2], s) * plan.piece + begin
            span = pl.ds(pl.multiple_of(start, 8), rows)
            copies.append(pltpu.make_async_copy(sources[s], out.at[pl.ds(ri, 1), span, :], sems.at[s]))
        for copy in copies:
            copy.start()
        for copy in copies:
            copy.wait()

    return pl.pallas_call(
        kernel,
        grid_spec=pltpu.PrefetchScalarGridSpec(
            num_scalar_prefetch=1,
            grid=(2,),
            in_specs=[pl.BlockSpec((1, rows, width), lambda ri, _: (ri, 0, 0))] * count
            + [pl.BlockSpec(memory_space=pl.ANY)] * len(given),
            out_specs=pl.BlockSpec(memory_space=pl.ANY),
            scratch_shapes=[pltpu.SemaphoreType.DMA((count,))],
        ),
        out_shape=jax.ShapeDtypeStruct((2, plan.rows_dev, width), f32),
        input_output_aliases={count + 1: 0} if given else {},
        compiler_params=params(),
        cost_estimate=pl.CostEstimate(flops=0, bytes_accessed=9 * 10**6, transcendentals=0),
        name="place_rows",
    )(scalars, *pieces, *given)


class Plan:
    def __init__(self, field_shape, depth, slabs):
        self.planes = depth
        self.slabs = slabs
        self.length = field_shape[-1]
        self.rows_dev = field_shape[-2]
        self.level = depth * 2
        self.cols_dev = self.length // self.level
        tiles = self.cols_dev // LANES
        self.chunks = [LANES] * tiles
        self.starts = [sum(self.chunks[:i]) for i in range(len(self.chunks))]
        self.piece = self.rows_dev // depth
        self.units = max(1, min(8, self.piece // 8))
        self.cuts = [1, 2, 3, 2] if self.units == 8 else [1] * self.units
        self.slab_tiles = 2 * self.rows_dev // LANES

    def place_of(self, tile):
        owner, inner = divmod(tile * LANES, self.cols_dev)
        part = max(i for i, start in enumerate(self.starts) if start <= inner)
        first = inner - self.starts[part]
        return owner, part, slice(first, first + LANES)


def swapped(value, axes, size, step):
    return lax.ppermute(value, axes, [(i, i ^ step) for i in range(size)])


def after(value, *others):
    return lax.optimization_barrier((value,) + others)[0]


def halving_steps(size):
    steps = []
    step = 1
    while step < size:
        steps.append(step)
        step = step * 2
    return steps


def scatter_step(value, axis, size, position, step, others):
    upper = jnp.bitwise_and(position, step) != 0
    half = value.shape[0] // 2
    kept = jnp.where(upper, value[half:], value[:half])
    given = jnp.where(upper, value[:half], value[half:])
    return kept + swapped(after(given, *others), axis, size, step)


def gather_step(value, axis, size, position, step, others):
    upper = jnp.bitwise_and(position, step) != 0
    other = swapped(after(value, *others), axis, size, step)
    return jnp.concatenate([jnp.where(upper, other, value), jnp.where(upper, value, other)])


def exchanged(value, axes):
    return lax.all_to_all(value, axes, 0, 0, tiled=True)


def per_device(field, hologram, defocus):
    depth, slabs = lax.axis_size("depth"), lax.axis_size("slab")
    plan = Plan(field.shape, depth, slabs)
    length = plan.length
    d, z, c = lax.axis_index("depth"), lax.axis_index("slab"), lax.axis_index("core")
    me = d * 2 + c
    order = (z * 2 + c) * depth + d
    n_order = slabs * 2 * depth
    ends = jnp.stack([(order == 0).astype(jnp.int32), (order == n_order - 1).astype(jnp.int32), d.astype(jnp.int32)])
    level_axes = ("depth", "core")

    forward, inverse = lane_tables()
    tables = {
        "forward": jnp.asarray(forward),
        "inverse": jnp.asarray(inverse),
        "twiddle": jnp.asarray(twiddle_table(length, 32)),
    }
    column_freqs = np.arange(32)[:, None] + 32 * np.arange(LANES)[None, :]
    cos, sin = chirp(defocus[0], column_freqs, length)
    transfer = jnp.stack([cos, -sin]) * (1.0 / length)

    ordered = jnp.concatenate([defocus] + [swapped(defocus, "depth", depth, s) for s in range(1, depth)])
    depths = ordered[jnp.bitwise_xor(jnp.arange(depth, dtype=jnp.int32), d)]

    own = field[:, 0]
    early = cut_rows(plan, own, 0, plan.cuts[0])
    own, early = lax.optimization_barrier((own, early))
    early, depths = lax.optimization_barrier((early, depths))
    held = [exchanged(early, "depth")]

    sent = column_pass(plan, own, tables, transfer)
    bases, freqs = slot_bases(length)
    cos, sin = chirp(depths[None, :, None], freqs[:, None, :], length)
    weights = jnp.stack([cos, sin], axis=2).reshape(16, 2 * depth, 2 * LANES)
    weights, bases, *sent = lax.optimization_barrier((weights, jnp.asarray(bases), *sent))
    high, low = slot_matrices(plan, bases, weights)

    slot_k = np.array([g + 4 * q for g in range(GROUPS) for q in range(4)])
    turns = (jnp.asarray(slot_k * plan.slab_tiles, jnp.int32) * z) % 32
    angle = turns.astype(f32) * (2.0 * math.pi / 32)
    unit = jnp.asarray(np.where(slot_k == 0, 1.0 / 32, 2.0 / 32), f32)
    phases = jnp.stack([jnp.cos(angle), -jnp.sin(angle), jnp.cos(angle) * unit, jnp.sin(angle) * unit])

    mine = lax.dynamic_slice_in_dim(hologram, me * plan.cols_dev, plan.cols_dev, 1)
    theirs = lax.dynamic_slice_in_dim(hologram, jnp.bitwise_xor(me, 1) * plan.cols_dev, plan.cols_dev, 1)
    theirs = swapped(theirs, "core", 2, 1)
    holos = jnp.where(c == 0, jnp.stack([mine, theirs]), jnp.stack([theirs, mine]))

    count = len(plan.chunks)

    def forward_stage(value, part, others):
        start = plan.starts[part]
        here = holos[:, :, start : start + plan.chunks[part]]
        return row_forward(plan, phases, after(value, *others), here, high, low)

    def backward_stage(value, part, others):
        return row_backward(plan, phases, after(value, *others), high, low)

    def sum_stage(function, step):
        return lambda value, part, others: function(value, "slab", slabs, z, step, others)

    halvings = halving_steps(slabs)
    stages = [forward_stage]
    stages += [sum_stage(scatter_step, step) for step in halvings]
    stages += [sum_stage(gather_step, step) for step in reversed(halvings)]
    stages += [backward_stage]

    queue = list(sent) + [None] * (len(plan.cuts) - 1)
    state = [None] * count
    before, back = [held[0]], []
    slot = 0
    while len(back) < count:
        others, before = before, []
        if queue:
            value = queue.pop(0)
            if value is None:
                value = cut_rows(plan, field[:, 0], sum(plan.cuts[: len(held)]), plan.cuts[len(held)])
                held.append(exchanged(after(value, *others), "depth"))
                before.append(held[-1])
            else:
                before.append(exchanged(after(value, *others), level_axes))
                if slot < count:
                    state[slot] = before[-1]
                else:
                    back.append(before[-1])
        for part in range(count):
            number = slot - (part + 1)
            if 0 <= number < len(stages):
                state[part] = stages[number](state[part], part, others)
                before.append(state[part])
                if number == len(stages) - 1:
                    queue.append(state[part])
        if slot == 0:
            before += [high, low]
        slot += 1

    held = jnp.concatenate(held, axis=2)
    cos, sin = chirp(depths[:, None, None], column_freqs[None], length)
    transfer = jnp.stack([cos, sin], axis=1) * (1.0 / length)
    moved = step_pass(plan, back, held, tables, transfer)

    all_axes = ("depth", "slab", "core")
    device_at = [(i % depth) * (slabs * 2) + i // depth for i in range(n_order)]
    downward = [(device_at[i], device_at[i + 1]) for i in range(n_order - 1)]
    above = lax.ppermute(moved[:, :, -1:], all_axes, downward)
    below = lax.ppermute(moved[:, :, :1], all_axes, [(b, a) for a, b in downward])
    tiles = plan.piece // 8
    first = max(1, tiles // 4)
    result = None
    for begin, steps in ((0, first), (first, tiles - first)):
        parts = shrink_pass(plan, ends, moved, above, below, begin, steps)
        parts = [parts[0]] + [swapped(parts[s], "depth", depth, s) for s in range(1, depth)]
        result = place_rows(plan, ends, parts, begin * 8, result)
    return result.reshape(field.shape)


def solution(mesh):
    depth, row = mesh.shape["depth"], mesh.shape["row"]
    split = Mesh(mesh.devices.reshape(depth, row // 2, 2), ("depth", "slab", "core"))
    rows = ("slab", "core")
    return jax.shard_map(
        per_device,
        mesh=split,
        in_specs=(P(None, "depth", rows, None), P(rows, None), P("depth")),
        out_specs=P(None, "depth", rows, None),
        check_vma=False,
    )
```

```python
import math

import jax
import jax.numpy as jnp
import numpy as np
from jax import lax
from jax.experimental import pallas as pl
from jax.experimental.pallas import tpu as pltpu
from jax.sharding import Mesh, PartitionSpec as P

tv_step_size = 1.0 / 12.0
tv_sharpness = 0.25
LANES = 128
GROUPS = 4
VMEM_BYTES = 60 * 1024 * 1024
f32 = jnp.float32
bf16 = jnp.bfloat16


def c_add(u, v):
    return (u[0] + v[0], u[1] + v[1])


def c_sub(u, v):
    return (u[0] - v[0], u[1] - v[1])


def c_rot(u, num, den):
    num = num % den
    if num == 0:
        return u
    if 4 * num == den:
        return (-u[1], u[0])
    if 2 * num == den:
        return (-u[0], -u[1])
    if 4 * num == 3 * den:
        return (u[1], -u[0])
    if (8 * num) % den == 0:
        half = math.sqrt(0.5)
        eighth = (8 * num) // den
        plus = (u[0] + u[1]) * half
        minus = (u[0] - u[1]) * half
        if eighth == 1:
            return (minus, plus)
        if eighth == 3:
            return (-plus, minus)
        if eighth == 5:
            return (-minus, -plus)
        return (plus, -minus)
    cos = math.cos(2 * math.pi * num / den)
    sin = math.sin(2 * math.pi * num / den)
    return (u[0] * cos - u[1] * sin, u[0] * sin + u[1] * cos)


def dft4(v, sign):
    s, d = c_add(v[0], v[2]), c_sub(v[0], v[2])
    t, u = c_add(v[1], v[3]), c_sub(v[1], v[3])
    u = c_rot(u, sign, 4)
    return [c_add(s, t), c_add(d, u), c_sub(s, t), c_sub(d, u)]


def dft8(v, sign):
    even, odd = dft4(v[0::2], sign), dft4(v[1::2], sign)
    odd = [c_rot(odd[q], sign * q, 8) for q in range(4)]
    return [c_add(even[q], odd[q]) for q in range(4)] + [c_sub(even[q], odd[q]) for q in range(4)]


def real_rot(value, num, den):
    cos = math.cos(2 * math.pi * num / den)
    sin = math.sin(2 * math.pi * num / den)
    return (value * cos, value * sin)


def total(values):
    out = values[0]
    for value in values[1:]:
        out = out + value
    return out


def slab_forward(x, group):
    count = len(x)
    if group == 0 and count == 8:
        s0, d0, s1, d1 = x[0] + x[4], x[0] - x[4], x[2] + x[6], x[2] - x[6]
        s2, d2, s3, d3 = x[1] + x[5], x[1] - x[5], x[3] + x[7], x[3] - x[7]
        e0, e2, o0, o2 = s0 + s1, s0 - s1, s2 + s3, s2 - s3
        p1 = c_rot((d2, -d3), -1, 8)
        p3 = c_rot((d2, d3), -3, 8)
        return [(e0 + o0, e0 - o0), (d0 + p1[0], p1[1] - d1), (e2, -o2), (d0 + p3[0], d1 + p3[1])]
    if count == 8:
        w = [(x[0], None)] + [real_rot(x[j], -group * j, 32) for j in range(1, 8)]
        s, d = (x[0] + w[4][0], w[4][1]), (x[0] - w[4][0], -w[4][1])
        t, u = c_add(w[2], w[6]), c_rot(c_sub(w[2], w[6]), -1, 4)
        even = [c_add(s, t), c_add(d, u), c_sub(s, t), c_sub(d, u)]
        odd = dft4(w[1::2], -1)
        return [c_add(even[q], c_rot(odd[q], -q, 8)) for q in range(4)]
    outs = []
    for q in range(4):
        parts = [real_rot(x[j], -(group + 4 * q) * j, 32) for j in range(count)]
        outs.append((total([v[0] for v in parts]), total([v[1] for v in parts])))
    if group == 0:
        outs[0] = (total(x), total([x[j] if j % 2 == 0 else -x[j] for j in range(count)]))
    return outs


def slab_inverse(g, group, count):
    if group == 0:
        (top, alt), rest = g[0], g[1:]
        if count == 8:
            (a1, b1), (a2, b2), (a3, b3) = rest
            half = math.sqrt(0.5)
            p, m = top + alt, top - alt
            s13, d13 = a1 + a3, b1 - b3
            x0, x4 = p + a2 + s13, p + a2 - s13
            x2, x6 = p - a2 - d13, p - a2 + d13
            u = (a1 - a3) * half
            v = (b1 + b3) * half
            x1, x5 = m - b2 + (u - v), m - b2 - (u - v)
            x3, x7 = m + b2 - (u + v), m + b2 + (u + v)
            return [x0, x1, x2, x3, x4, x5, x6, x7]
        outs = []
        for j in range(count):
            terms = [c_rot(rest[q - 1], q * j, 8)[0] for q in range(1, 4)]
            outs.append((top + alt if j % 2 == 0 else top - alt) + total(terms))
        return outs
    if count == 8:
        even = dft4(g, 1)
        odd = dft4([c_rot(g[q], q, 8) for q in range(4)], 1)
        v = [even[0], odd[0], even[1], odd[1], even[2], odd[2], even[3], odd[3]]
        outs = [v[0][0]]
        for j in range(1, 8):
            cos = math.cos(2 * math.pi * group * j / 32)
            sin = math.sin(2 * math.pi * group * j / 32)
            outs.append(v[j][0] * cos - v[j][1] * sin)
        return outs
    outs = []
    for j in range(count):
        terms = [c_rot(g[q], (group + 4 * q) * j, 32)[0] for q in range(4)]
        outs.append(total(terms))
    return outs


def two_parts(value):
    high = value.astype(bf16)
    low = (value - high.astype(f32)).astype(bf16)
    return high, low


def dot(left, right):
    return jnp.dot(left, right, preferred_element_type=f32)


def host_parts(matrix):
    high = matrix.astype(np.float32).astype(jnp.bfloat16)
    low = (matrix - high.astype(np.float64)).astype(np.float32).astype(jnp.bfloat16)
    return high, low


def lane_tables():
    n = np.arange(LANES)
    angle = 2 * np.pi * (n[:, None] * n[None, :] % LANES) / LANES
    cos, sin = np.cos(angle), np.sin(angle)
    forward = np.block([[cos, -sin], [sin, cos]])
    inverse = np.block([[cos, sin], [-sin, cos]])
    stacked = []
    for matrix in (forward, inverse):
        high, low = host_parts(matrix)
        stacked.append(np.concatenate([high, high, low], axis=0))
    return stacked


def twiddle_table(length, tiles):
    k = np.arange(tiles)[:, None]
    n = np.arange(LANES)[None, :]
    angle = -2 * np.pi * (k * n % length) / length
    return np.stack([np.cos(angle), np.sin(angle)]).astype(np.float32)


def slot_bases(length):
    n = np.arange(LANES)[:, None]
    bases = np.zeros((16, 2 * LANES, 2 * LANES))
    freqs = np.zeros((16, 2 * LANES), np.int64)
    for group in range(GROUPS):
        for q in range(4):
            k = group + 4 * q
            slot = group * 4 + q
            if k == 0:
                column = 0
                for half, start in ((0, 0), (1, 16)):
                    rows = slice(half * LANES, (half + 1) * LANES)
                    for step in range(LANES // 2 + 1):
                        a = start + 32 * step
                        if a > length // 2:
                            continue
                        angle = 2 * np.pi * (a * n[:, 0] % length) / length
                        if a in (0, length // 2):
                            bases[slot, rows, column] = np.cos(angle) / np.sqrt(LANES)
                            freqs[slot, column] = a
                            column += 1
                            continue
                        bases[slot, rows, column] = np.cos(angle) * np.sqrt(2 / LANES)
                        bases[slot, rows, column + 1] = np.sin(angle) * np.sqrt(2 / LANES)
                        freqs[slot, column : column + 2] = a
                        column += 2
                assert column == 2 * LANES
                continue
            a = k + 32 * np.arange(LANES)[None, :]
            angle = 2 * np.pi * (a * n % length) / length
            cos, sin = np.cos(angle) / np.sqrt(LANES), np.sin(angle) / np.sqrt(LANES)
            bases[slot] = np.block([[cos, -sin], [sin, cos]])
            freqs[slot] = np.concatenate([a[0], a[0]])
    return bases.astype(np.float32), freqs


def chirp(depth_values, freqs, length):
    centred = np.where(freqs < length // 2, freqs, freqs - length)
    squares = (centred.astype(np.int64) ** 2).astype(np.int64)
    coarse = (squares // 2048 * 2048).astype(np.float32)
    fine = (squares % 2048).astype(np.float32)
    unit = 0.5 / (float(length) * float(length))
    whole = jnp.floor(depth_values * 2.0) * 0.5
    rest = depth_values - whole

    def turn(left, right):
        value = left * right * unit
        return value - jnp.floor(value)

    turns = turn(whole, coarse) + turn(whole, fine) + rest * (coarse * unit) + rest * (fine * unit)
    angle = (turns - jnp.floor(turns)) * (2.0 * math.pi)
    return jnp.cos(angle), jnp.sin(angle)


def lane_convolve(rows, load, store, scratch, forward_ref, inverse_ref, twiddle_ref, transfer):
    ahead, behind = scratch[0], scratch[1]
    parts, spec = scratch[2:4], scratch[4:6]

    def twiddle(tile):
        return twiddle_ref[0, tile : tile + 1, :], twiddle_ref[1, tile : tile + 1, :]

    def forward(chunk):
        row, out = chunk * 16, parts[chunk % 2]
        for b in range(8):
            x = [load(8 * a + b, row) for a in range(4)]
            y = dft4(x, -1)
            for k in range(4):
                v = c_rot(y[k], -b * k, 32)
                ahead[0, k * 8 + b] = v[0]
                ahead[1, k * 8 + b] = v[1]
        for k in range(4):
            y = dft8([(ahead[0, k * 8 + b], ahead[1, k * 8 + b]) for b in range(8)], -1)
            for m in range(8):
                tile = k + 4 * m
                tr, ti = twiddle(tile)
                re, im = y[m]
                span = slice(tile * 16, tile * 16 + 16)
                for at, value in enumerate((re * tr - im * ti, re * ti + im * tr)):
                    high, low = two_parts(value)
                    out[span, at * LANES : (at + 1) * LANES] = high
                    out[span, (2 + at) * LANES : (3 + at) * LANES] = low
                    out[span, (4 + at) * LANES : (5 + at) * LANES] = high

    def middle(chunk):
        taken, out = parts[chunk % 2], spec[chunk % 2]
        for first in range(0, 32, 16):
            span = slice(first * 16, first * 16 + 256)
            value = dot(taken[span, :], forward_ref[...])
            pieces = []
            for t in range(16):
                tr, ti = transfer(first + t)
                re, im = value[t * 16 : t * 16 + 16, :LANES], value[t * 16 : t * 16 + 16, LANES:]
                pieces.append(jnp.concatenate([re * tr - im * ti, re * ti + im * tr], axis=1))
            high, low = two_parts(jnp.concatenate(pieces, axis=0))
            out[span, :] = dot(jnp.concatenate([high, low, high], axis=1), inverse_ref[...])

    def inverse(chunk):
        row, taken = chunk * 16, spec[chunk % 2]
        for k in range(4):
            x = []
            for m in range(8):
                tile = k + 4 * m
                tr, ti = twiddle(tile)
                span = slice(tile * 16, tile * 16 + 16)
                re, im = taken[span, :LANES], taken[span, LANES:]
                x.append((re * tr + im * ti, im * tr - re * ti))
            y = dft8(x, 1)
            for b in range(8):
                v = c_rot(y[b], b * k, 32)
                behind[0, k * 8 + b] = v[0]
                behind[1, k * 8 + b] = v[1]
        for b in range(8):
            y = dft4([(behind[0, k * 8 + b], behind[1, k * 8 + b]) for k in range(4)], 1)
            for a in range(4):
                store(8 * a + b, row, y[a])

    count = rows // 16
    for t in range(count + 2):
        if t < count:
            forward(t)
        if 0 <= t - 1 < count:
            middle(t - 1)
        if 0 <= t - 2 < count:
            inverse(t - 2)


def lane_scratch():
    work = pltpu.VMEM((2, 32, 16, LANES), f32)
    parts = pltpu.VMEM((512, 6 * LANES), bf16)
    spec = pltpu.VMEM((512, 2 * LANES), f32)
    return [work, work, parts, parts, spec, spec]


def params():
    return pltpu.CompilerParams(vmem_limit_bytes=VMEM_BYTES)


def whole_block(array):
    rank = array.ndim
    return pl.BlockSpec(array.shape, lambda *_: (0,) * rank)


def column_pass(plan, field, tables, transfer):
    rows = min(64, plan.rows_dev)
    level, count = plan.level, len(plan.chunks)

    def kernel(f_ref, fwd, inv, twd, tra, *rest):
        outs, scratch = rest[:count], rest[count:]

        def load(tile, row):
            at = slice(tile * LANES, (tile + 1) * LANES)
            return (f_ref[0, pl.ds(row, 16), at], f_ref[1, pl.ds(row, 16), at])

        def store(tile, row, value):
            owner, part, at = plan.place_of(tile)
            outs[part][owner, 0, pl.ds(row, 16), at] = value[0]
            outs[part][owner, 1, pl.ds(row, 16), at] = value[1]

        def pick(tile):
            return tra[0, tile : tile + 1, :], tra[1, tile : tile + 1, :]

        lane_convolve(rows, load, store, scratch, fwd, inv, twd, pick)

    width = field.shape[-1]
    fixed = [tables["forward"], tables["inverse"], tables["twiddle"], transfer]
    return pl.pallas_call(
        kernel,
        grid=(plan.rows_dev // rows,),
        in_specs=[pl.BlockSpec((2, rows, width), lambda i: (0, i, 0))] + [whole_block(a) for a in fixed],
        out_specs=[pl.BlockSpec((level, 2, rows, w), lambda i: (0, 0, i, 0)) for w in plan.chunks],
        scratch_shapes=lane_scratch(),
        out_shape=[jax.ShapeDtypeStruct((level, 2, plan.rows_dev, w), f32) for w in plan.chunks],
        compiler_params=params(),
        cost_estimate=pl.CostEstimate(flops=13 * 10**9, bytes_accessed=34 * 10**6, transcendentals=0),
        name="column_pass",
    )(field, *fixed)


def cut_rows(plan, field, first, count):
    width = field.shape[-1]
    rows, units = plan.piece // plan.units, plan.units

    def kernel(x_ref, out_ref):
        out_ref[0] = x_ref[...]

    return pl.pallas_call(
        kernel,
        grid=(plan.planes, count),
        in_specs=[pl.BlockSpec((2, rows, width), lambda p, u: (0, p * units + first + u, 0))],
        out_specs=pl.BlockSpec((1, 2, rows, width), lambda p, u: (p, 0, u, 0)),
        out_shape=jax.ShapeDtypeStruct((plan.planes, 2, rows * count, width), f32),
        compiler_params=params(),
        cost_estimate=pl.CostEstimate(flops=0, bytes_accessed=9 * 10**6, transcendentals=0),
        name="cut_rows",
    )(field)


def slot_matrices(plan, bases, weights):
    kinds = weights.shape[1]
    size = 2 * LANES

    def kernel(b_ref, w_ref, high_ref, low_ref):
        basis = b_ref[0]
        for kind in range(kinds):
            scaled = basis * w_ref[0, kind : kind + 1, :]
            product = lax.dot_general(
                scaled,
                basis,
                (((1,), (1,)), ((), ())),
                precision=lax.Precision.HIGHEST,
                preferred_element_type=f32,
            )
            high, low = two_parts(product)
            high_ref[0, :, kind * size : (kind + 1) * size] = high
            low_ref[0, :, kind * size : (kind + 1) * size] = low

    shape = jax.ShapeDtypeStruct((16, size, kinds * size), bf16)
    return pl.pallas_call(
        kernel,
        grid=(16,),
        in_specs=[
            pl.BlockSpec((1, size, size), lambda i: (i, 0, 0)),
            pl.BlockSpec((1, kinds, size), lambda i: (i, 0, 0)),
        ],
        out_specs=[pl.BlockSpec((1, size, kinds * size), lambda i: (i, 0, 0))] * 2,
        out_shape=[shape, shape],
        compiler_params=params(),
        cost_estimate=pl.CostEstimate(flops=26 * 10**9, bytes_accessed=34 * 10**6, transcendentals=0),
        name="slot_matrices",
    )(bases, weights)


def row_forward(plan, phases, pieces, holos, high, low):
    count = plan.slab_tiles
    chunk = pieces.shape[-1]
    kinds = plan.planes * 2
    size = 2 * LANES
    half = count // 2

    def kernel(phase, x_ref, h_ref, wh, wl, out, eh, el, eo):
        for group in range(GROUPS):

            @pl.when(pl.program_id(0) == group)
            def _(group=group):
                def rows_of(i, carry):
                    row = i * 16
                    for kind in range(kinds):
                        t, ri = kind // 2, kind % 2

                        x = []
                        for j in range(count):
                            span = pl.ds((j % half) * LANES + row, 16)
                            x.append(x_ref[2 * t + j // half, ri, span, :])
                        outs = slab_forward(x, group)
                        for q in range(4):
                            for at in range(2):
                                a, b = two_parts(outs[q][at])
                                span = pl.ds(kind * size + at * LANES + row, 16)
                                eh[q, span, :] = a
                                el[q, span, :] = b
                    x = []
                    for j in range(count):
                        span = pl.ds((j % half) * LANES + row, 16)
                        x.append(h_ref[j // half, span, :])
                    held = slab_forward(x, group)
                    for q in range(4):
                        for at in range(2):
                            eo[q, pl.ds(at * LANES + row, 16), :] = held[q][at]
                    return carry

                lax.fori_loop(0, LANES // 16, rows_of, 0)

        for q in range(4):
            value = dot(wh[q], eh[q]) + dot(wh[q], el[q]) + dot(wl[q], eh[q]) - eo[q]
            slot = pl.program_id(0) * 4 + q
            cos, sin = phase[0, slot], phase[1, slot]
            re, im = value[:LANES], value[LANES:]
            out[q, :LANES, :] = re * cos - im * sin
            out[q, LANES:, :] = re * sin + im * cos

    return pl.pallas_call(
        kernel,
        grid_spec=pltpu.PrefetchScalarGridSpec(
            num_scalar_prefetch=1,
            grid=(GROUPS,),
            in_specs=[whole_block(pieces), whole_block(holos)]
            + [pl.BlockSpec((4, size, kinds * size), lambda g, *_: (g, 0, 0))] * 2,
            out_specs=pl.BlockSpec((4, size, chunk), lambda g, *_: (g, 0, 0)),
            scratch_shapes=[
                pltpu.VMEM((4, kinds * size, chunk), bf16),
                pltpu.VMEM((4, kinds * size, chunk), bf16),
                pltpu.VMEM((4, size, chunk), f32),
            ],
        ),
        out_shape=jax.ShapeDtypeStruct((16, size, chunk), f32),
        compiler_params=params(),
        cost_estimate=pl.CostEstimate(flops=13 * 10**9, bytes_accessed=60 * 10**6, transcendentals=0),
        name="row_forward",
    )(phases, pieces, holos, high, low)


def row_backward(plan, phases, misfit, high, low):
    level, count = plan.level, plan.slab_tiles
    chunk = misfit.shape[-1]
    size = 2 * LANES
    piece = plan.piece

    def kernel(phase, m_ref, wh, wl, out, mh, ml, field):
        kind, step = pl.program_id(0), pl.program_id(1)

        @pl.when(kind == 0)
        def _():
            for q in range(4):
                slot = step * 4 + q
                cos, sin = phase[2, slot], phase[3, slot]
                re, im = m_ref[q, :LANES, :], m_ref[q, LANES:, :]
                for at, value in enumerate((re * cos - im * sin, re * sin + im * cos)):
                    a, b = two_parts(value)
                    mh[slot, at * LANES : (at + 1) * LANES, :] = a
                    ml[slot, at * LANES : (at + 1) * LANES, :] = b

        grads = []
        for q in range(4):
            slot = step * 4 + q
            grads.append(dot(wh[q], mh[slot]) + dot(wh[q], ml[slot]) + dot(wl[q], mh[slot]))
        for group in range(GROUPS):

            @pl.when(step == group)
            def _(group=group):
                for row in range(0, LANES, 16):
                    g = [(v[row : row + 16], v[LANES + row : LANES + row + 16]) for v in grads]
                    values = slab_inverse(g, group, count)
                    for j in range(count):
                        span = pl.ds(j * LANES + row, 16)
                        if group == 0:
                            field[span, :] = values[j]
                        else:
                            field[span, :] = field[span, :] + values[j]

        @pl.when(step == GROUPS - 1)
        def _():
            for s in range(level):
                start = (s % 2) * plan.rows_dev + (s // 2) * piece
                out[s, 0] = field[start : start + piece, :]

    kinds = plan.planes * 2

    return pl.pallas_call(
        kernel,
        grid_spec=pltpu.PrefetchScalarGridSpec(
            num_scalar_prefetch=1,
            grid=(kinds, GROUPS),
            in_specs=[
                pl.BlockSpec((4, size, chunk), lambda kind, step, _: (jnp.where(kind == 0, step, GROUPS - 1), 0, 0)),
                pl.BlockSpec((4, size, size), lambda kind, step, _: (step, 0, kind)),
                pl.BlockSpec((4, size, size), lambda kind, step, _: (step, 0, kind)),
            ],
            out_specs=pl.BlockSpec((level, 1, piece, chunk), lambda kind, step, _: (0, kind, 0, 0)),
            scratch_shapes=[
                pltpu.VMEM((16, size, chunk), bf16),
                pltpu.VMEM((16, size, chunk), bf16),
                pltpu.VMEM((count * LANES, chunk), f32),
            ],
        ),
        out_shape=jax.ShapeDtypeStruct((level, kinds, piece, chunk), f32),
        compiler_params=params(),
        cost_estimate=pl.CostEstimate(flops=13 * 10**9, bytes_accessed=60 * 10**6, transcendentals=0),
        name="row_backward",
    )(phases, misfit, high, low)


def step_pass(plan, pieces, held, tables, transfer):
    rows = min(64, plan.piece)
    level, count = plan.level, len(plan.chunks)
    width = held.shape[-1]
    scale = 1.0 / plan.planes

    def kernel(*refs):
        g_refs, (h_ref, fwd, inv, twd, tra, out), scratch = refs[:count], refs[count : count + 6], refs[count + 6 :]

        def load(tile, row):
            owner, part, at = plan.place_of(tile)
            return (g_refs[part][owner, 0, pl.ds(row, 16), at], g_refs[part][owner, 1, pl.ds(row, 16), at])

        def store(tile, row, value):
            at = slice(tile * LANES, (tile + 1) * LANES)
            for ri in range(2):
                before = h_ref[0, ri, pl.ds(row, 16), at]
                out[0, ri, pl.ds(row, 16), at] = before - scale * value[ri]

        def pick(tile):
            return tra[0, 0, tile : tile + 1, :], tra[0, 1, tile : tile + 1, :]

        lane_convolve(rows, load, store, scratch, fwd, inv, twd, pick)

    fixed = [tables["forward"], tables["inverse"], tables["twiddle"]]
    return pl.pallas_call(
        kernel,
        grid=(plan.planes, plan.piece // rows),
        in_specs=[pl.BlockSpec((level, 2, rows, w), lambda p, i: (0, p, i, 0)) for w in plan.chunks]
        + [pl.BlockSpec((1, 2, rows, width), lambda p, i: (p, 0, i, 0))]
        + [whole_block(a) for a in fixed]
        + [pl.BlockSpec((1, 2, 32, LANES), lambda p, i: (p, 0, 0, 0))],
        out_specs=pl.BlockSpec((1, 2, rows, width), lambda p, i: (p, 0, i, 0)),
        scratch_shapes=lane_scratch(),
        out_shape=jax.ShapeDtypeStruct((plan.planes, 2, plan.piece, width), f32),
        compiler_params=params(),
        cost_estimate=pl.CostEstimate(flops=13 * 10**9, bytes_accessed=51 * 10**6, transcendentals=0),
        name="step_pass",
    )(*pieces, held, *fixed, transfer)


def shrink_pass(plan, scalars, moved, above, below, begin, steps):
    planes, width = plan.planes, moved.shape[-1]
    tiles = plan.piece // 8
    at_top, at_bottom = begin == 0, begin + steps == tiles
    cols = 1024

    def kernel(scal, cur, nxt, up, down, *rest):
        outs, (carry, est) = rest[:planes], rest[planes:]
        i = pl.program_id(0)
        last = jnp.logical_and(i == steps - 1, at_bottom)
        row_ids = lax.broadcasted_iota(jnp.int32, (8, cols), 0)
        lane_ids = lax.broadcasted_iota(jnp.int32, (8, cols), 1)
        end_row = jnp.logical_and(last, scal[1] != 0)

        def flux(tile, next_row, p, start):
            at_end = start + cols == width
            here = [tile(p, ri, start, cols) for ri in range(2)]
            dz, dy, dx = [], [], []
            for ri in range(2):
                if p + 1 < planes:
                    dz.append(tile(p + 1, ri, start, cols) - here[ri])
                follow = jnp.where(row_ids == 7, next_row(p, ri, start), pltpu.roll(here[ri], 7, 0))
                dy.append(follow - here[ri])
                if at_end:
                    ahead = jnp.where(lane_ids == cols - 1, here[ri], pltpu.roll(here[ri], cols - 1, 1))
                else:
                    joined = jnp.concatenate([here[ri], tile(p, ri, start + cols, LANES)], axis=1)
                    ahead = pltpu.roll(joined, cols + LANES - 1, 1)[:, :cols]
                dx.append(ahead - here[ri])
            squares = [v * v for v in dz + dy + dx]
            magnitude = jnp.sqrt(total(squares))
            factor = 1.0 / (1.0 + tv_sharpness * magnitude)
            return here, [v * factor for v in dz], [v * factor for v in dy], [v * factor for v in dx]

        @pl.when(i == 0)
        def _():
            for p in range(planes):
                for start in range(0, width, cols):
                    def tile(p, ri, at, wide):
                        line = slice(0, 1) if at_top else slice(7, 8)
                        return jnp.broadcast_to(up[p, ri, line, at : at + wide], (8, wide))

                    def next_row(p, ri, at):
                        return cur[p, ri, 0:1, at : at + cols]

                    fy = flux(tile, next_row, p, start)[2]
                    for ri in range(2):
                        if at_top:
                            fy[ri] = jnp.where(scal[0] != 0, 0.0, fy[ri])
                        carry[p, ri, :, start : start + cols] = fy[ri]

        def tile(p, ri, at, wide):
            return cur[p, ri, :, at : at + wide]

        def next_row(p, ri, at):
            inner = nxt[p, ri, 0:1, at : at + cols]
            outer = down[p, ri, 0:1, at : at + cols]
            own = cur[p, ri, 7:8, at : at + cols]
            return jnp.where(end_row, own, jnp.where(last, outer, inner))

        prior_x = {}
        for start in range(0, width, cols):
            prior_z = None
            for p in range(planes):
                here, fz, fy, fx = flux(tile, next_row, p, start)
                for ri in range(2):
                    behind_y = jnp.where(row_ids == 0, carry[p, ri, 7:8, start : start + cols], pltpu.roll(fy[ri], 1, 0))
                    if start == 0:
                        behind_x = jnp.where(lane_ids == 0, 0.0, pltpu.roll(fx[ri], 1, 1))
                    else:
                        joined = jnp.concatenate([prior_x[p, ri], fx[ri]], axis=1)
                        behind_x = pltpu.roll(joined, 1, 1)[:, LANES:]
                    divergence = (fy[ri] - behind_y) + (fx[ri] - behind_x)
                    if fz:
                        divergence = divergence + fz[ri]
                    if prior_z:
                        divergence = divergence - prior_z[ri]
                    est[p, ri, :, start : start + cols] = here[ri] + tv_step_size * divergence
                    carry[p, ri, :, start : start + cols] = fy[ri]
                    prior_x[p, ri] = fx[ri][:, cols - LANES :]
                prior_z = fz
        for s in range(planes):
            outs[s][...] = est[jnp.bitwise_xor(scal[2], s)]
    return pl.pallas_call(
        kernel,
        grid_spec=pltpu.PrefetchScalarGridSpec(
            num_scalar_prefetch=1,
            grid=(steps,),
            in_specs=[
                pl.BlockSpec((planes, 2, 8, width), lambda i, _: (0, 0, begin + i, 0)),
                pl.BlockSpec((planes, 2, 8, width), lambda i, _: (0, 0, jnp.minimum(begin + i + 1, tiles - 1), 0)),
                whole_block(above) if at_top else pl.BlockSpec((planes, 2, 8, width), lambda i, _: (0, 0, begin - 1, 0)),
                whole_block(below),
            ],
            out_specs=[pl.BlockSpec((2, 8, width), lambda i, _: (0, i, 0))] * planes,
            scratch_shapes=[
                pltpu.VMEM((planes, 2, 8, width), f32),
                pltpu.VMEM((planes, 2, 8, width), f32),
            ],
        ),
        out_shape=[jax.ShapeDtypeStruct((2, steps * 8, width), f32)] * planes,
        compiler_params=params(),
        cost_estimate=pl.CostEstimate(flops=10**8, bytes_accessed=9 * 10**6, transcendentals=10**6),
        name="shrink_pass",
    )(scalars, moved, moved, above if at_top else moved, below)


def place_rows(plan, scalars, pieces, begin, result):
    rows, width = pieces[0].shape[-2:]
    count = len(pieces)
    given = [] if result is None else [result]

    def kernel(scal, *refs):
        sources, out, sems = refs[:count], refs[count + len(given)], refs[-1]
        ri = pl.program_id(0)
        copies = []
        for s in range(count):
            start = jnp.bitwise_xor(scal[2], s) * plan.piece + begin
            span = pl.ds(pl.multiple_of(start, 8), rows)
            copies.append(pltpu.make_async_copy(sources[s], out.at[pl.ds(ri, 1), span, :], sems.at[s]))
        for copy in copies:
            copy.start()
        for copy in copies:
            copy.wait()

    return pl.pallas_call(
        kernel,
        grid_spec=pltpu.PrefetchScalarGridSpec(
            num_scalar_prefetch=1,
            grid=(2,),
            in_specs=[pl.BlockSpec((1, rows, width), lambda ri, _: (ri, 0, 0))] * count
            + [pl.BlockSpec(memory_space=pl.ANY)] * len(given),
            out_specs=pl.BlockSpec(memory_space=pl.ANY),
            scratch_shapes=[pltpu.SemaphoreType.DMA((count,))],
        ),
        out_shape=jax.ShapeDtypeStruct((2, plan.rows_dev, width), f32),
        input_output_aliases={count + 1: 0} if given else {},
        compiler_params=params(),
        cost_estimate=pl.CostEstimate(flops=0, bytes_accessed=9 * 10**6, transcendentals=0),
        name="place_rows",
    )(scalars, *pieces, *given)


class Plan:
    def __init__(self, field_shape, depth, slabs):
        self.planes = depth
        self.slabs = slabs
        self.length = field_shape[-1]
        self.rows_dev = field_shape[-2]
        self.level = depth * 2
        self.cols_dev = self.length // self.level
        tiles = self.cols_dev // LANES
        self.chunks = [LANES] * tiles
        self.starts = [sum(self.chunks[:i]) for i in range(len(self.chunks))]
        self.piece = self.rows_dev // depth
        self.units = max(1, min(8, self.piece // 8))
        self.cuts = [1, 2, 3, 2] if self.units == 8 else [1] * self.units
        self.slab_tiles = 2 * self.rows_dev // LANES

    def place_of(self, tile):
        owner, inner = divmod(tile * LANES, self.cols_dev)
        part = max(i for i, start in enumerate(self.starts) if start <= inner)
        first = inner - self.starts[part]
        return owner, part, slice(first, first + LANES)


def swapped(value, axes, size, step):
    return lax.ppermute(value, axes, [(i, i ^ step) for i in range(size)])


def after(value, *others):
    return lax.optimization_barrier((value,) + others)[0]


def halving_steps(size):
    steps = []
    step = 1
    while step < size:
        steps.append(step)
        step = step * 2
    return steps


def scatter_step(value, axis, size, position, step, others):
    upper = jnp.bitwise_and(position, step) != 0
    half = value.shape[0] // 2
    kept = jnp.where(upper, value[half:], value[:half])
    given = jnp.where(upper, value[:half], value[half:])
    return kept + swapped(after(given, *others), axis, size, step)


def gather_step(value, axis, size, position, step, others):
    upper = jnp.bitwise_and(position, step) != 0
    other = swapped(after(value, *others), axis, size, step)
    return jnp.concatenate([jnp.where(upper, other, value), jnp.where(upper, value, other)])


def exchanged(value, axes):
    return lax.all_to_all(value, axes, 0, 0, tiled=True)


def per_device(field, hologram, defocus):
    depth, slabs = lax.axis_size("depth"), lax.axis_size("slab")
    plan = Plan(field.shape, depth, slabs)
    length = plan.length
    d, z, c = lax.axis_index("depth"), lax.axis_index("slab"), lax.axis_index("core")
    me = d * 2 + c
    order = (z * 2 + c) * depth + d
    n_order = slabs * 2 * depth
    ends = jnp.stack([(order == 0).astype(jnp.int32), (order == n_order - 1).astype(jnp.int32), d.astype(jnp.int32)])
    level_axes = ("depth", "core")

    forward, inverse = lane_tables()
    tables = {
        "forward": jnp.asarray(forward),
        "inverse": jnp.asarray(inverse),
        "twiddle": jnp.asarray(twiddle_table(length, 32)),
    }
    column_freqs = np.arange(32)[:, None] + 32 * np.arange(LANES)[None, :]
    cos, sin = chirp(defocus[0], column_freqs, length)
    transfer = jnp.stack([cos, -sin]) * (1.0 / length)

    ordered = jnp.concatenate([defocus] + [swapped(defocus, "depth", depth, s) for s in range(1, depth)])
    depths = ordered[jnp.bitwise_xor(jnp.arange(depth, dtype=jnp.int32), d)]

    own = field[:, 0]
    early = cut_rows(plan, own, 0, plan.cuts[0])
    own, early = lax.optimization_barrier((own, early))
    early, depths = lax.optimization_barrier((early, depths))
    held = [exchanged(early, "depth")]

    sent = column_pass(plan, own, tables, transfer)
    bases, freqs = slot_bases(length)
    cos, sin = chirp(depths[None, :, None], freqs[:, None, :], length)
    weights = jnp.stack([cos, sin], axis=2).reshape(16, 2 * depth, 2 * LANES)
    weights, bases, *sent = lax.optimization_barrier((weights, jnp.asarray(bases), *sent))
    high, low = slot_matrices(plan, bases, weights)

    slot_k = np.array([g + 4 * q for g in range(GROUPS) for q in range(4)])
    turns = (jnp.asarray(slot_k * plan.slab_tiles, jnp.int32) * z) % 32
    angle = turns.astype(f32) * (2.0 * math.pi / 32)
    unit = jnp.asarray(np.where(slot_k == 0, 1.0 / 32, 2.0 / 32), f32)
    phases = jnp.stack([jnp.cos(angle), -jnp.sin(angle), jnp.cos(angle) * unit, jnp.sin(angle) * unit])

    mine = lax.dynamic_slice_in_dim(hologram, me * plan.cols_dev, plan.cols_dev, 1)
    theirs = lax.dynamic_slice_in_dim(hologram, jnp.bitwise_xor(me, 1) * plan.cols_dev, plan.cols_dev, 1)
    theirs = swapped(theirs, "core", 2, 1)
    holos = jnp.where(c == 0, jnp.stack([mine, theirs]), jnp.stack([theirs, mine]))

    count = len(plan.chunks)

    def forward_stage(value, part, others):
        start = plan.starts[part]
        here = holos[:, :, start : start + plan.chunks[part]]
        return row_forward(plan, phases, after(value, *others), here, high, low)

    def backward_stage(value, part, others):
        return row_backward(plan, phases, after(value, *others), high, low)

    def sum_stage(function, step):
        return lambda value, part, others: function(value, "slab", slabs, z, step, others)

    halvings = halving_steps(slabs)
    stages = [forward_stage]
    stages += [sum_stage(scatter_step, step) for step in halvings]
    stages += [sum_stage(gather_step, step) for step in reversed(halvings)]
    stages += [backward_stage]

    queue = list(sent) + [None] * (len(plan.cuts) - 1)
    state = [None] * count
    before, back, cuts = [held[0]], [], []
    slot = 0
    while len(back) < count:
        others, before = before, []
        if queue:
            value = queue.pop(0)
            if value is None:
                held.append(exchanged(after(cuts[len(held) - 1], *others), "depth"))
                before.append(held[-1])
            else:
                before.append(exchanged(after(value, *others), level_axes))
                if slot < count:
                    state[slot] = before[-1]
                else:
                    back.append(before[-1])
        for part in range(count):
            number = slot - (part + 1)
            if 0 <= number < len(stages):
                state[part] = stages[number](state[part], part, others)
                before.append(state[part])
                if number == len(stages) - 1:
                    queue.append(state[part])
        if slot == 0:
            before += [high, low]
        if slot + 1 < len(plan.cuts):
            cuts.append(cut_rows(plan, field[:, 0], sum(plan.cuts[: slot + 1]), plan.cuts[slot + 1]))
            before.append(cuts[-1])
        slot += 1

    held = jnp.concatenate(held, axis=2)
    cos, sin = chirp(depths[:, None, None], column_freqs[None], length)
    transfer = jnp.stack([cos, sin], axis=1) * (1.0 / length)
    moved = step_pass(plan, back, held, tables, transfer)

    all_axes = ("depth", "slab", "core")
    device_at = [(i % depth) * (slabs * 2) + i // depth for i in range(n_order)]
    downward = [(device_at[i], device_at[i + 1]) for i in range(n_order - 1)]
    above = lax.ppermute(moved[:, :, -1:], all_axes, downward)
    below = lax.ppermute(moved[:, :, :1], all_axes, [(b, a) for a, b in downward])
    tiles = plan.piece // 8
    first = max(1, tiles // 4)
    result = None
    for begin, steps in ((0, first), (first, tiles - first)):
        if result is not None:
            moved = after(moved, parts[0])
        parts = shrink_pass(plan, ends, moved, above, below, begin, steps)
        parts = [parts[0]] + [swapped(parts[s], "depth", depth, s) for s in range(1, depth)]
        result = place_rows(plan, ends, parts, begin * 8, result)
    return result.reshape(field.shape)


def solution(mesh):
    depth, row = mesh.shape["depth"], mesh.shape["row"]
    split = Mesh(mesh.devices.reshape(depth, row // 2, 2), ("depth", "slab", "core"))
    rows = ("slab", "core")
    return jax.shard_map(
        per_device,
        mesh=split,
        in_specs=(P(None, "depth", rows, None), P(rows, None), P("depth")),
        out_specs=P(None, "depth", rows, None),
        check_vma=False,
    )
```
